128 devices in a mesh: loop: 32 (over z_lo, y, x), grp: 4 (over z_hi, core).
Axes of the slice: x: 4, y: 4, z: 4 (z_hi: 2, z_lo: 2; z = z_hi * 2 + z_lo), core: 2. Of those that a mesh axis runs over, the one named last changes fastest.
Arguments:
- inputs: bfloat16 [2, 128, 4096], P(None, 'grp', 'loop'), may hold values from -6 to 6
- in_weight: bfloat16 [4096, 12304], P('loop', 'grp'), may hold values from -0.09375 to 0.09375
- gate_bias: float32 [2, 8], replicated, may hold values from -2 to 104, as said below
- memory: float32 [128, 8, 256, 512], P(('grp', 'loop')), may hold values from -6 to 6
- normalizer: float32 [128, 8, 256], P(('grp', 'loop')), may hold values from -6 to 6
- stabilizer: float32 [128, 8], P(('grp', 'loop')), may hold values from 0 to 4
- out_gain: float32 [4096], replicated, may hold values from 0.5 to 1.5
- out_weight: bfloat16 [4096, 4096], P(None, 'loop'), may hold values from -0.09375 to 0.09375
Outputs:
- mixed_out: bfloat16 [2, 128, 4096], P(None, 'grp', 'loop')
- memory_out: float32 [128, 8, 256, 512], P(('grp', 'loop'))
- normalizer_out: float32 [128, 8, 256], P(('grp', 'loop'))
- stabilizer_out: float32 [128, 8], P(('grp', 'loop'))
The draws below stay inside these ranges and needn't reach their ends.
Inputs may be any that keep to these rules, and one draw needn't show every extreme that they name: `gate_bias`: row 0 holds the input gates' biases, row 1 the forget gates'.
All inputs are finite; a program needn't handle non-finite values.
Results may differ from the reference program's by a relative error of at most 0.005.
Values may be sent and summed in bfloat16 or wider, within the bound.
A program may use at most 64 MiB of HBM per device.

```python
import math
import jax
import jax.numpy as jnp
from jax import lax

D = 4096
HEADS = 8
QK_DIM = 256
V_DIM = 512
DRAFTS = 2
REQ = 128
PROJ = 12304


def draw_gate_bias(key, part):
    key = jax.random.fold_in(key, 7)
    admit_key, forget_key = jax.random.split(key)
    forget_row = jax.random.uniform(forget_key, (1, HEADS), jnp.float32, 0.5, 6.0)
    admit_row = jax.random.uniform(admit_key, (1, HEADS), jnp.float32, -2.0, 2.0)
    return jnp.concatenate([admit_row, forget_row], 0)


def block_scale(key, extent, cuts, low, largest):
    def one(dim, parts):
        draws = jax.random.uniform(jax.random.fold_in(jax.random.fold_in(key, 6), dim), (parts,), jnp.float32, low / len(cuts), largest / len(cuts))
        return jnp.repeat(jnp.exp(draws), extent[dim] // parts).reshape((-1,) + (1,) * (len(extent) - dim - 1))

    gain = one(*cuts[0])
    for cut in cuts[1:]:
        gain = gain * one(*cut)
    return gain


def bell_draw(stream_key, dims, deviation, reach, shards=(), held_as=jnp.bfloat16):
    entries = jax.random.normal(stream_key, dims, jnp.float32) * deviation
    if len(shards) > 0:
        entries = block_scale(stream_key, dims, shards, -0.22, 0.18) * entries
    return jnp.clip(entries, min=-reach, max=reach).astype(held_as)


def setup_inputs(seed: int = 0) -> dict:
    streams_of = jax.random.split(jax.random.key(seed), 9)
    return {
        "inputs": bell_draw(streams_of[0], (DRAFTS, REQ, D), 1.0, 6.0, ((1, 4), (2, 32))),
        "in_weight": bell_draw(streams_of[1], (D, PROJ), D ** -0.5, 0.09375, ((0, 32), (1, 4))),
        "gate_bias": draw_gate_bias(jax.random.fold_in(streams_of[8], 71), 0),
        "memory": bell_draw(streams_of[3], (REQ, HEADS, QK_DIM, V_DIM), 1.0, 6.0, ((0, 128),), jnp.float32),
        "normalizer": bell_draw(streams_of[4], (REQ, HEADS, QK_DIM), 1.0, 6.0, ((0, 128),), jnp.float32),
        "stabilizer": jnp.clip(4.0 * jax.random.uniform(streams_of[5], (REQ, HEADS), jnp.float32) ** block_scale(streams_of[5], (REQ, HEADS), ((0, 128),), -0.2, 0.2), 0.0, 4.0),
        "out_gain": jnp.clip(1.0 + 0.1 * jax.random.normal(streams_of[6], (D,), jnp.float32), 0.5, 1.5),
        "out_weight": bell_draw(streams_of[7], (D, D), D ** -0.5, 0.09375, ((1, 32),)),
    }


def advance(current, step_row, gate_bias, out_gain):
    memory, normalizer, stabilizer = current
    requests = memory.shape[0]
    head_count = memory.shape[1]
    key_dim = memory.shape[2]
    value_dim = memory.shape[3]
    qk_width = head_count * key_dim
    model_width = head_count * value_dim
    queries = step_row[:, :qk_width].reshape(requests, head_count, key_dim)
    keys = (step_row[:, qk_width:2 * qk_width] * (1.0 / math.sqrt(key_dim))).reshape(requests, head_count, key_dim)
    base = 2 * qk_width
    values = step_row[:, base:base + model_width].reshape(requests, head_count, value_dim)
    out_gate = step_row[:, base + model_width:base + 2 * model_width]
    gates = base + 2 * model_width
    admit_pre = step_row[:, gates:gates + head_count] + gate_bias[0]
    forget_pre = step_row[:, gates + head_count:gates + 2 * head_count] + gate_bias[1]
    log_forget = jax.nn.log_sigmoid(forget_pre)
    new_stabilizer = jnp.maximum(log_forget + stabilizer, admit_pre)
    forget = jnp.exp(log_forget + stabilizer - new_stabilizer)
    admit = jnp.exp(admit_pre - new_stabilizer)
    scaled_keys = admit[..., None] * keys
    memory = forget[..., None, None] * memory + scaled_keys[..., :, None] * values[..., None, :]
    normalizer = forget[..., None] * normalizer + scaled_keys
    numerator = jnp.einsum('rhk,rhkv->rhv', queries, memory, precision=lax.Precision.HIGHEST)
    denominator = jnp.maximum(jnp.abs(lax.optimization_barrier(jnp.sum(queries * normalizer, -1))), 1.0)
    hidden = (numerator / denominator[..., None]).reshape(requests, model_width)
    rescale = lax.rsqrt(lax.optimization_barrier(jnp.mean(hidden * hidden, -1, keepdims=True)) + 1e-06)
    readout = (hidden * rescale * out_gain * jax.nn.sigmoid(out_gate)).astype(jnp.bfloat16)
    return ((memory, normalizer, new_stabilizer), readout)

def reference(inputs, in_weight, gate_bias, memory, normalizer, stabilizer, out_gain, out_weight):
    steps_total = inputs.shape[0]
    requests = inputs.shape[1]
    width = inputs.shape[2]
    flat = jnp.dot(inputs.reshape(steps_total * requests, width), in_weight, preferred_element_type=jnp.float32)
    per_request = jnp.swapaxes(flat.reshape(steps_total, requests, in_weight.shape[1]), 0, 1)

    def single(operands):
        memory_one, normalizer_one, stabilizer_one, rows_one = operands

        def stepper(current, step_row):
            return advance(current, step_row[None], gate_bias, out_gain)
        start_state = (memory_one[None], normalizer_one[None], stabilizer_one[None])
        finished, readouts = lax.scan(stepper, start_state, rows_one)
        return ((finished[0][0], finished[1][0], finished[2][0]), readouts[:, 0])
    finished, readouts = lax.map(single, (memory, normalizer, stabilizer, per_request))
    product = jnp.dot(readouts.reshape(requests * steps_total, width), out_weight, preferred_element_type=jnp.float32)
    mixed_out = jnp.swapaxes(product.reshape(requests, steps_total, width), 0, 1).astype(jnp.bfloat16)
    return (mixed_out, finished[0], finished[1], finished[2])
```

```python
import jax
import jax.numpy as jnp
from jax import lax
from jax.experimental import pallas as pl
from jax.experimental.pallas import tpu as pltpu
from jax.sharding import PartitionSpec as P

MESH = pl.DeviceIdType.MESH
F32 = jnp.float32
BF16 = jnp.bfloat16


def split_low(value):
    return value - value.astype(BF16).astype(F32)


def to_column(row, shift=0):
    wide = jnp.broadcast_to(row, (8, row.shape[1]))
    lane = lax.broadcasted_iota(jnp.int32, wide.shape, 1)
    head = lax.broadcasted_iota(jnp.int32, wide.shape, 0)
    return jnp.sum(jnp.where(lane == head + shift, wide, 0.0), axis=1, keepdims=True)


def exchange_kernel(
    inputs_hbm, weight_hbm, bias_hbm, memory_hbm, norm_hbm, stab_hbm, gain_hbm, out_weight_hbm,
    mixed_ref, memory_out_ref, norm_out_ref, stab_out_ref,
    stage, memory, out_weight, bias, norm, stab, gain, rows_in, rows, tail, tail_f32, weights,
    send_f32, send, received, tiles, rolled, flat, numer, scaled, readout, gathered, gathered_f32, left,
    load_sem, own_sem, rows_send, rows_sem, ring_send, ring_sem, tail_send, tail_sem, w_send, w_sem, pass_send,
    pass_sem, sums_send, sums_recv, gather_send, gather_recv, ping_sem,
):
    loop_id = lax.axis_index("loop")
    grp_id = lax.axis_index("grp")
    x = lax.rem(loop_id, 4)
    y = lax.rem(lax.div(loop_id, 4), 4)
    z_lo = lax.div(loop_id, 16)
    z_hi = lax.div(grp_id, 2)
    core = lax.rem(grp_id, 2)

    def x_peer(o):
        return (z_lo * 16 + y * 4 + lax.rem(x + o, 4), grp_id)

    def y_peer(o):
        return (z_lo * 16 + lax.rem(y + o, 4) * 4 + x, grp_id)

    z_peer = (loop_id, (1 - z_hi) * 2 + core)
    other_lo = (1 - z_lo) * 16 + y * 4 + x
    z_near = [(other_lo, grp_id), (other_lo, (1 - z_hi) * 2 + core)]
    sibling = (loop_id, z_hi * 2 + 1 - core)

    loads = [
        pltpu.make_async_copy(src, dst, load_sem.at[i])
        for i, (src, dst) in enumerate((
            (inputs_hbm, rows_in.at[z_hi]),
            (weight_hbm, stage),
            (bias_hbm, bias),
            (stab_hbm, stab),
            (norm_hbm.at[0], norm),
            (gain_hbm, gain),
            (memory_hbm.at[0], memory),
            (out_weight_hbm, out_weight),
        ))
    ]
    for load in loads:
        load.start()

    barrier = pltpu.get_barrier_semaphore()
    peers = [x_peer(2), y_peer(2), z_peer] + z_near
    peers += [x_peer(1), x_peer(3), y_peer(1), y_peer(3), sibling]
    for peer in peers:
        pl.semaphore_signal(barrier, inc=1, device_id=peer, device_id_type=MESH)

    loads[0].wait()
    loads[1].wait()
    tail_f32[...] = jnp.zeros_like(tail_f32)
    tail_f32[0:4, :] = stage[3072:3076, :].astype(F32)
    tail[0] = pltpu.roll(tail_f32[...], grp_id * 4, 0).astype(BF16)

    pl.semaphore_wait(barrier, len(peers))

    def remote(src, dst, send_sem, recv_sem, peer):
        copy = pltpu.make_async_remote_copy(
            src_ref=src, dst_ref=dst, send_sem=send_sem, recv_sem=recv_sem, device_id=peer, device_id_type=MESH
        )
        copy.start()
        return copy

    def wait_bytes(ref, sem):
        pltpu.make_async_copy(ref, ref, sem).wait()

    rows_copy = remote(rows_in.at[z_hi], rows_in.at[z_hi], rows_send, rows_sem, z_peer)
    for peer in z_near:
        pl.semaphore_signal(ping_sem, inc=1, device_id=peer, device_id_type=MESH)
    tail_pair = remote(tail.at[0], tail.at[1], tail_send.at[0], tail_sem.at[0], sibling)

    def pieces(kind, holder, slot):
        wide = pl.ds(pl.multiple_of(kind * 1024 + holder * 256, 128), 256)
        one = pl.ds(pl.multiple_of(2048 + kind * 512 + holder * 128, 128), 128)
        deep = pl.ds(slot * 128, 128)
        return (
            (stage.at[wide], weights.at[kind, core, pl.ds(0, 256), deep]),
            (stage.at[one], weights.at[kind, core, pl.ds(256, 128), deep]),
        )

    for o in (2, 1, 3):
        for kind, coord, peer in ((0, x, x_peer(o)), (1, y, y_peer(o))):
            for src, dst in pieces(kind, lax.rem(coord + o, 4), 4 - o):
                remote(src, dst, w_send, w_sem.at[kind, 4 - o], peer)
    for kind, coord in ((0, x), (1, y)):
        for src, dst in pieces(kind, coord, 0):
            pltpu.make_async_copy(src, dst, own_sem).start()
            remote(src, dst, pass_send, pass_sem, sibling)

    tail_pair.wait_recv()
    tail[2] = tail[0] + tail[1]
    tail_all = remote(tail.at[2], tail.at[3], tail_send.at[1], tail_sem.at[1], z_peer)

    rows_copy.wait_recv()
    pl.semaphore_wait(ping_sem, 2)
    for o in (2, 1, 3):
        remote(rows_in, rows.at[4 - o], ring_send, ring_sem, x_peer(o))
        remote(rows_in, rows.at[8 - o], ring_send, ring_sem, y_peer(o))
    rows_own = rows_in[...].reshape(128, 128)
    tail_all.wait_recv()
    tail_columns = jnp.concatenate([tail[2] + tail[3], jnp.zeros((112, 128), BF16)], axis=0)
    across = (((1,), (1,)), ((), ()))
    tail_part = lax.dot_general(rows_own, tail_columns, across, preferred_element_type=F32)

    for slot in (3, 1, 2):
        for kind in range(2):
            block = weights.at[kind, core, :, pl.ds(slot * 128, 128)]
            wait_bytes(block, w_sem.at[kind, slot])
            remote(block, block, pass_send, pass_sem, sibling)
    wait_bytes(weights.at[0, 0, :, pl.ds(0, 256)], own_sem)
    wait_bytes(rows.at[pl.ds(0, 6)], ring_sem)
    wait_bytes(weights.at[0], pass_sem)

    def store(j, value):
        for half in range(2):
            for draft in range(2):
                start = half * 1024 + draft * 16 + j
                first = half * 64 + draft * 32
                send_f32[pl.ds(start, 32, stride=32), :] = value[first : first + 32]

    in_low = z_hi == 0
    for index in range(2):
        lhs = jnp.concatenate([rows_own] + [rows[index * 4 + s].reshape(128, 128) for s in (1, 2, 3)], axis=1)
        for side in range(2):
            part = lax.dot_general(lhs, weights[index, side], across, preferred_element_type=F32)
            for t in range(3):
                store(index * 6 + side * 3 + t, part[:, t * 128 : (t + 1) * 128])
            if side == 0:
                low = [split_low(part[:, t * 128 : (t + 1) * 128]) for t in range(2)]
                if index == 0:
                    low_x = low
                else:
                    low_y = low
            elif index == 1:
                low_gates = split_low(part[:, 256:384])
    store(12, jnp.where(in_low, low_x[0], low_gates))
    store(13, jnp.where(in_low, low_x[1], tail_part))
    store(14, jnp.where(in_low, low_y[0], split_low(tail_part)))
    store(15, low_y[1])
    for block in range(8):
        send[pl.ds(block * 8, 8)] = send_f32[pl.ds(block * 256, 256), :].astype(BF16).reshape(8, 32, 128)

    me = z_hi * 32 + loop_id

    def send_sums(i, _):
        owner = lax.rem(me + i, 64)
        pltpu.make_async_remote_copy(
            src_ref=send.at[owner], dst_ref=received.at[me], send_sem=sums_send, recv_sem=sums_recv,
            device_id=(lax.rem(owner, 32), lax.div(owner, 32) * 2 + core), device_id_type=MESH,
        ).start()
        return 0

    lax.fori_loop(1, 64, send_sums, 0)
    keep = pltpu.make_async_copy(send.at[me], received.at[me], own_sem)
    keep.start()

    for load in loads[2:]:
        load.wait()
    keep.wait()
    wait_bytes(received.at[pl.ds(0, 63)], sums_recv)

    tails = None
    for half in range(2):
        for holder in range(4):
            sum_x = sum_y = None
            for lo in range(2):
                for k in range(4):
                    one_x = received[half * 32 + lo * 16 + k * 4 + holder].astype(F32)
                    one_y = received[half * 32 + lo * 16 + holder * 4 + k].astype(F32)
                    sum_x = one_x if sum_x is None else sum_x + one_x
                    sum_y = one_y if sum_y is None else sum_y + one_y
            if half == 1:
                tails = sum_x if tails is None else tails + sum_x
            for draft in range(2):
                b = draft * 16
                for index, total in enumerate((sum_x, sum_y)):
                    for side in range(2):
                        j = b + index * 6 + side * 3
                        pair, last = total[j : j + 2], total[j + 2 : j + 3]
                        if half == 0 and side == 0:
                            pair = pair + total[b + 12 + index * 2 : b + 14 + index * 2]
                        if half == 1 and side == 1 and index == 1 and holder == 3:
                            last = last + total[b + 12 : b + 13]
                        base = half * 48 + side * 24
                        tiles[draft, pl.ds(base + index * 8 + 2 * holder, 2), :] = pair
                        tiles[draft, pl.ds(base + 16 + index * 4 + holder, 1), :] = last

    lane = lax.broadcasted_iota(jnp.int32, (24, 128), 1)
    row = lax.broadcasted_iota(jnp.int32, (24, 128), 0)
    gate_rows = []
    for draft in range(2):
        tail_row = tails[draft * 16 + 13 : draft * 16 + 14] + tails[draft * 16 + 14 : draft * 16 + 15]
        for grp in range(4):
            block = tiles[draft, pl.ds(grp * 24, 24), :]
            if grp:
                block = pltpu.roll(block, 4 * grp, 1)
            rolled[draft, pl.ds(grp * 24 + 1, 24), :] = block
            if grp:
                before = rolled[draft, pl.ds(grp * 24, 24), :]
                merged = jnp.where(lane >= 4 * grp, block, before)
                edge = (row == 0) & (lane >= 4 * grp - 4) & (lane < 4 * grp)
                block_out = jnp.where(edge, jnp.broadcast_to(tail_row, (24, 128)), merged)
            else:
                block_out = block
            flat[draft, pl.ds(grp * 24, 24), :] = block_out
        last = rolled[draft, pl.ds(96, 1), :]
        gate_rows.append(jnp.where(lane[0:1] >= 12, tail_row, last))

    queries_t = jnp.concatenate([flat[0, 0:16, :], flat[1, 0:16, :]], axis=0).T
    for head in range(8):
        totals = [jnp.zeros((8, 512), F32), jnp.zeros((8, 512), F32)]
        for part in range(8):
            block = memory[head, pl.ds(part * 32, 32), :]
            k = (part % 4) * 32
            for draft in range(2):
                at = draft * 16 + head * 2 + part // 4
                product = queries_t[k : k + 32, at : at + 1] * block
                totals[draft] = totals[draft] + jnp.sum(product.reshape(4, 8, 512), axis=0)
        for draft in range(2):
            numer[draft, pl.ds(head, 1), :] = jnp.sum(totals[draft], axis=0, keepdims=True)

    def by_head(draft, first, width):
        return [flat[draft, pl.ds(first + i, 8, stride=width), :] for i in range(width)]

    def dot(a, b):
        total = a[0] * b[0]
        for i in range(1, len(a)):
            total = total + a[i] * b[i]
        return jnp.sum(total, axis=1, keepdims=True)

    q = [by_head(d, 0, 2) for d in range(2)]
    keys = [[k * 0.0625 for k in by_head(d, 16, 2)] for d in range(2)]
    v = [by_head(d, 32, 4) for d in range(2)]
    out_gate = [by_head(d, 64, 4) for d in range(2)]
    n_old = [norm[:, 0:128], norm[:, 128:256]]
    admit_bias = to_column(bias[0:1, :])
    forget_bias = to_column(bias[1:2, :])
    stabilizer = to_column(stab[...])
    forget, admit = [], []
    for draft in range(2):
        admit_pre = to_column(gate_rows[draft]) + admit_bias
        forget_pre = to_column(gate_rows[draft], 8) + forget_bias
        log_forget = jnp.minimum(forget_pre, 0.0) - jnp.log1p(jnp.exp(-jnp.abs(forget_pre)))
        new_stabilizer = jnp.maximum(log_forget + stabilizer, admit_pre)
        forget.append(jnp.exp(log_forget + stabilizer - new_stabilizer))
        admit.append(jnp.exp(admit_pre - new_stabilizer))
        stabilizer = new_stabilizer
    square = (8, 8)
    diagonal = lax.broadcasted_iota(jnp.int32, square, 0) == lax.broadcasted_iota(jnp.int32, square, 1)
    stab_out_ref[...] = jnp.sum(
        jnp.where(diagonal, jnp.broadcast_to(stabilizer, square), 0.0), axis=0, keepdims=True
    )
    f0, f1, a0, a1 = forget[0], forget[1], admit[0], admit[1]
    q0k0, q1k0, q1k1 = dot(q[0], keys[0]), dot(q[1], keys[0]), dot(q[1], keys[1])
    den0 = f0 * dot(q[0], n_old) + a0 * q0k0
    den1 = f1 * (f0 * dot(q[1], n_old) + a0 * q1k0) + a1 * q1k1
    inverse = [1.0 / jnp.maximum(jnp.abs(den0), 1.0), 1.0 / jnp.maximum(jnp.abs(den1), 1.0)]
    for i in range(2):
        norm_out_ref[0, :, pl.ds(i * 128, 128)] = f1 * (f0 * n_old[i] + a0 * keys[0][i]) + a1 * keys[1][i]

    messages = []
    for draft in range(2):
        hidden = []
        for j in range(4):
            old = numer[draft, :, pl.ds(j * 128, 128)]
            if draft == 0:
                top = f0 * old + (a0 * q0k0) * v[0][j]
            else:
                top = f1 * (f0 * old + (a0 * q1k0) * v[0][j]) + (a1 * q1k1) * v[1][j]
            hidden.append(top * inverse[draft])
        square_sum = hidden[0] * hidden[0]
        for j in range(1, 4):
            square_sum = square_sum + hidden[j] * hidden[j]
        mean = jnp.sum(jnp.sum(square_sum, axis=1, keepdims=True), axis=0, keepdims=True) * (1.0 / 4096.0)
        rescale = lax.rsqrt(mean + 1e-06)
        for j in range(4):
            gain_j = gain[pl.ds(j, 8, stride=4), :]
            messages.append(hidden[j] * rescale * gain_j * jax.nn.sigmoid(out_gate[draft][j]))
    readout[...] = jnp.concatenate(messages, axis=0).astype(BF16)

    def send_readout(i, _):
        to = lax.rem(loop_id + i, 32)
        pltpu.make_async_remote_copy(
            src_ref=readout, dst_ref=gathered.at[loop_id], send_sem=gather_send, recv_sem=gather_recv,
            device_id=(to, grp_id), device_id_type=MESH,
        ).start()
        return 0

    lax.fori_loop(1, 32, send_readout, 0)
    keep = pltpu.make_async_copy(readout, gathered.at[loop_id], own_sem)
    keep.start()

    for j in range(4):
        scaled[0, :, pl.ds(j * 128, 128)] = (f1 * a0) * v[0][j]
        scaled[1, :, pl.ds(j * 128, 128)] = a1 * v[1][j]
    keys_t = (jnp.concatenate([flat[0, 16:32, :], flat[1, 16:32, :]], axis=0) * 0.0625).T
    kept = f1 * f0
    for head in range(8):
        fade = jnp.broadcast_to(kept[head : head + 1, :], (32, 512))
        row0, row1 = scaled[0, pl.ds(head, 1), :], scaled[1, pl.ds(head, 1), :]
        for part in range(8):
            k = (part % 4) * 32
            at = head * 2 + part // 4
            k0 = keys_t[k : k + 32, at : at + 1]
            k1 = keys_t[k : k + 32, 16 + at : 17 + at]
            old = memory[head, pl.ds(part * 32, 32), :]
            memory_out_ref[0, head, pl.ds(part * 32, 32), :] = fade * old + k0 * row0 + k1 * row1

    keep.wait()
    wait_bytes(gathered.at[pl.ds(0, 31)], gather_recv)

    for block in range(8):
        gathered_f32[pl.ds(block * 256, 256), :] = gathered[pl.ds(block * 4, 4)].reshape(256, 128).astype(F32)
    for draft in range(2):
        for j in range(4):
            for head in range(8):
                piece = gathered_f32[pl.ds(draft * 32 + j * 8 + head, 32, stride=64), :]
                left[pl.ds(draft * 32, 32), pl.ds((head * 4 + j) * 128, 128)] = piece.astype(BF16)
    product = jnp.dot(left[...], out_weight[...], preferred_element_type=F32)
    mixed_ref[...] = product.astype(BF16).reshape(2, 32, 128)

    rows_copy.wait_send()
    tail_pair.wait_send()
    tail_all.wait_send()
    wait_bytes(weights.at[0, :, :, pl.ds(0, 384)], w_send)
    wait_bytes(weights.at[0], pass_send)
    wait_bytes(rows.at[pl.ds(0, 6)], ring_send)
    wait_bytes(send.at[pl.ds(0, 63)], sums_send)
    wait_bytes(gathered.at[pl.ds(0, 31)], gather_send)


def body(inputs, in_weight, gate_bias, memory, normalizer, stabilizer, out_gain, out_weight):
    vmem = pl.BlockSpec(memory_space=pltpu.VMEM)
    hbm = pl.BlockSpec(memory_space=pltpu.HBM)
    dma = pltpu.SemaphoreType.DMA
    out_shape = (
        jax.ShapeDtypeStruct((2, 32, 128), BF16),
        jax.ShapeDtypeStruct(memory.shape, F32),
        jax.ShapeDtypeStruct((1, 8, 256), F32),
        jax.ShapeDtypeStruct((1, 8), F32),
    )
    return pl.pallas_call(
        exchange_kernel,
        out_shape=out_shape,
        in_specs=[hbm] * 8,
        out_specs=(vmem,) * 4,
        scratch_shapes=[
            pltpu.VMEM((3076, 128), BF16),
            pltpu.VMEM((8, 256, 512), F32),
            pltpu.VMEM((4096, 128), BF16),
            pltpu.VMEM((2, 8), F32),
            pltpu.VMEM((8, 256), F32),
            pltpu.VMEM((1, 8), F32),
            pltpu.VMEM((32, 128), F32),
            pltpu.VMEM((2, 2, 32, 128), BF16),
            pltpu.VMEM((8, 2, 2, 32, 128), BF16),
            pltpu.VMEM((4, 16, 128), BF16),
            pltpu.VMEM((16, 128), F32),
            pltpu.VMEM((2, 2, 384, 512), BF16),
            pltpu.VMEM((2048, 128), F32),
            pltpu.VMEM((64, 32, 128), BF16),
            pltpu.VMEM((64, 32, 128), BF16),
            pltpu.VMEM((2, 96, 128), F32),
            pltpu.VMEM((2, 104, 128), F32),
            pltpu.VMEM((2, 96, 128), F32),
            pltpu.VMEM((2, 8, 512), F32),
            pltpu.VMEM((2, 8, 512), F32),
            pltpu.VMEM((64, 128), BF16),
            pltpu.VMEM((32, 64, 128), BF16),
            pltpu.VMEM((2048, 128), F32),
            pltpu.VMEM((64, 4096), BF16),
            dma((8,)),
            dma,
            dma,
            dma,
            dma,
            dma,
            dma((2,)),
            dma((2,)),
            dma,
            dma((2, 4)),
            dma,
            dma,
            dma,
            dma,
            dma,
            dma,
            pltpu.SemaphoreType.REGULAR,
        ],
        compiler_params=pltpu.CompilerParams(
            collective_id=0, has_side_effects=True, vmem_limit_bytes=40 * 2**20
        ),
    )(*(
        pltpu.with_memory_space_constraint(operand, pltpu.HBM)
        for operand in (
            inputs, in_weight.T, gate_bias, memory, normalizer, stabilizer, out_gain.reshape(32, 128), out_weight
        )
    ))


def solution(mesh):
    in_specs = (
        P(None, "grp", "loop"),
        P("loop", "grp"),
        P(),
        P(("grp", "loop"), None, None, None),
        P(("grp", "loop"), None, None),
        P(("grp", "loop"), None),
        P(),
        P(None, "loop"),
    )
    out_specs = (
        P(None, "grp", "loop"),
        P(("grp", "loop"), None, None, None),
        P(("grp", "loop"), None, None),
        P(("grp", "loop"), None),
    )
    return jax.shard_map(body, mesh=mesh, in_specs=in_specs, out_specs=out_specs, check_vma=False)
```

```python
import jax
import jax.numpy as jnp
from jax import lax
from jax.experimental import pallas as pl
from jax.experimental.pallas import tpu as pltpu
from jax.sharding import PartitionSpec as P

MESH = pl.DeviceIdType.MESH
F32 = jnp.float32
BF16 = jnp.bfloat16


def split_low(value):
    return value - value.astype(BF16).astype(F32)


def offsets(deep):
    steps = [(o_z, o_y, o_x) for o_z in range(deep) for o_y in range(4) for o_x in range(4)]
    return sorted(steps[1:], key=lambda step: -sum(min(o, 4 - o) for o in step))


def to_column(row, shift=0):
    wide = jnp.broadcast_to(row, (8, row.shape[1]))
    lane = lax.broadcasted_iota(jnp.int32, wide.shape, 1)
    head = lax.broadcasted_iota(jnp.int32, wide.shape, 0)
    return jnp.sum(jnp.where(lane == head + shift, wide, 0.0), axis=1, keepdims=True)


def exchange_kernel(
    inputs_hbm, weight_hbm, bias_hbm, memory_hbm, norm_hbm, stab_hbm, gain_hbm, out_weight_hbm,
    mixed_ref, memory_out_ref, norm_out_ref, stab_out_ref,
    stage, memory, out_weight, bias, norm, stab, gain, rows_in, rows, tail, tail_f32, weights,
    send_f32, send, received, tiles, rolled, flat, numer, scaled, readout, gathered, gathered_f32, left,
    load_sem, own_sem, rows_send, rows_sem, ring_send, ring_sem, tail_send, tail_sem, w_send, w_sem, pass_send,
    pass_sem, sums_send, sums_recv, gather_send, gather_recv, ping_sem,
):
    loop_id = lax.axis_index("loop")
    grp_id = lax.axis_index("grp")
    x = lax.rem(loop_id, 4)
    y = lax.rem(lax.div(loop_id, 4), 4)
    z_lo = lax.div(loop_id, 16)
    z_hi = lax.div(grp_id, 2)
    core = lax.rem(grp_id, 2)

    def x_peer(o):
        return (z_lo * 16 + y * 4 + lax.rem(x + o, 4), grp_id)

    def y_peer(o):
        return (z_lo * 16 + lax.rem(y + o, 4) * 4 + x, grp_id)

    z_peer = (loop_id, (1 - z_hi) * 2 + core)
    other_lo = (1 - z_lo) * 16 + y * 4 + x
    z_near = [(other_lo, grp_id), (other_lo, (1 - z_hi) * 2 + core)]
    sibling = (loop_id, z_hi * 2 + 1 - core)

    loads = [
        pltpu.make_async_copy(src, dst, load_sem.at[i])
        for i, (src, dst) in enumerate((
            (inputs_hbm, rows_in.at[z_hi]),
            (weight_hbm, stage),
            (bias_hbm, bias),
            (stab_hbm, stab),
            (norm_hbm.at[0], norm),
            (gain_hbm, gain),
            (memory_hbm.at[0], memory),
            (out_weight_hbm, out_weight),
        ))
    ]
    for load in loads:
        load.start()

    barrier = pltpu.get_barrier_semaphore()
    peers = [x_peer(2), y_peer(2), z_peer] + z_near
    peers += [x_peer(1), x_peer(3), y_peer(1), y_peer(3), sibling]
    for peer in peers:
        pl.semaphore_signal(barrier, inc=1, device_id=peer, device_id_type=MESH)

    loads[0].wait()
    loads[1].wait()
    tail_f32[...] = jnp.zeros_like(tail_f32)
    tail_f32[0:4, :] = stage[3072:3076, :].astype(F32)
    tail[0] = pltpu.roll(tail_f32[...], grp_id * 4, 0).astype(BF16)

    pl.semaphore_wait(barrier, len(peers))

    def remote(src, dst, send_sem, recv_sem, peer):
        copy = pltpu.make_async_remote_copy(
            src_ref=src, dst_ref=dst, send_sem=send_sem, recv_sem=recv_sem, device_id=peer, device_id_type=MESH
        )
        copy.start()
        return copy

    def wait_bytes(ref, sem):
        pltpu.make_async_copy(ref, ref, sem).wait()

    rows_copy = remote(rows_in.at[z_hi], rows_in.at[z_hi], rows_send, rows_sem, z_peer)
    for peer in z_near:
        pl.semaphore_signal(ping_sem, inc=1, device_id=peer, device_id_type=MESH)
    tail_pair = remote(tail.at[0], tail.at[1], tail_send.at[0], tail_sem.at[0], sibling)

    def pieces(kind, holder, slot):
        wide = pl.ds(pl.multiple_of(kind * 1024 + holder * 256, 128), 256)
        one = pl.ds(pl.multiple_of(2048 + kind * 512 + holder * 128, 128), 128)
        deep = pl.ds(slot * 128, 128)
        return (
            (stage.at[wide], weights.at[kind, core, pl.ds(0, 256), deep]),
            (stage.at[one], weights.at[kind, core, pl.ds(256, 128), deep]),
        )

    for o in (2, 1, 3):
        for kind, coord, peer in ((0, x, x_peer(o)), (1, y, y_peer(o))):
            for src, dst in pieces(kind, lax.rem(coord + o, 4), 4 - o):
                remote(src, dst, w_send, w_sem.at[kind, 4 - o], peer)
    for kind, coord in ((0, x), (1, y)):
        for src, dst in pieces(kind, coord, 0):
            pltpu.make_async_copy(src, dst, own_sem).start()
            remote(src, dst, pass_send, pass_sem, sibling)

    tail_pair.wait_recv()
    tail[2] = tail[0] + tail[1]
    tail_all = remote(tail.at[2], tail.at[3], tail_send.at[1], tail_sem.at[1], z_peer)

    rows_copy.wait_recv()
    pl.semaphore_wait(ping_sem, 2)
    for o in (2, 1, 3):
        remote(rows_in, rows.at[4 - o], ring_send, ring_sem, x_peer(o))
        remote(rows_in, rows.at[8 - o], ring_send, ring_sem, y_peer(o))
    rows_own = rows_in[...].reshape(128, 128)
    tail_all.wait_recv()
    tail_columns = jnp.concatenate([tail[2] + tail[3], jnp.zeros((112, 128), BF16)], axis=0)
    across = (((1,), (1,)), ((), ()))
    tail_part = lax.dot_general(rows_own, tail_columns, across, preferred_element_type=F32)

    for slot in (3, 1, 2):
        for kind in range(2):
            block = weights.at[kind, core, :, pl.ds(slot * 128, 128)]
            wait_bytes(block, w_sem.at[kind, slot])
            remote(block, block, pass_send, pass_sem, sibling)
    wait_bytes(weights.at[0, 0, :, pl.ds(0, 256)], own_sem)
    wait_bytes(rows.at[pl.ds(0, 6)], ring_sem)
    wait_bytes(weights.at[0], pass_sem)

    parts = [
        [
            lax.dot_general(lhs, weights[kind, side], across, preferred_element_type=F32)
            for side in range(2)
        ]
        for kind in range(2)
        for lhs in [jnp.concatenate([rows_own] + [rows[kind * 4 + s].reshape(128, 128) for s in (1, 2, 3)], axis=1)]
    ]
    columns = [
        parts[kind][side][:, t * 128 : (t + 1) * 128] for kind in range(2) for side in range(2) for t in range(3)
    ]
    in_low = z_hi == 0
    columns += [
        jnp.where(in_low, split_low(columns[0]), split_low(columns[11])),
        jnp.where(in_low, split_low(columns[1]), tail_part),
        jnp.where(in_low, split_low(columns[6]), split_low(tail_part)),
        split_low(columns[7]),
    ]
    me = z_hi * 32 + loop_id
    for draft in range(2):
        for j, value in enumerate(columns):
            for half in range(2):
                first = half * 64 + draft * 32
                send_f32[pl.ds(half * 512 + j, 32, stride=16), :] = value[first : first + 32]
        for block in range(4):
            packed = send_f32[pl.ds(block * 256, 256), :].astype(BF16)
            send[draft, pl.ds(block * 16, 16)] = packed.reshape(16, 16, 128)
        for o_z, o_y, o_x in offsets(4):
            to = lax.rem(z_lo * 16 + z_hi * 32 + o_z * 16, 64) + lax.rem(y + o_y, 4) * 4 + lax.rem(x + o_x, 4)
            pltpu.make_async_remote_copy(
                src_ref=send.at[draft, to], dst_ref=received.at[draft, me],
                send_sem=sums_send.at[draft], recv_sem=sums_recv.at[draft],
                device_id=(lax.rem(to, 32), lax.div(to, 32) * 2 + core), device_id_type=MESH,
            ).start()
    keep = pltpu.make_async_copy(send.at[:, me], received.at[:, me], own_sem)
    keep.start()

    for load in loads[2:]:
        load.wait()
    keep.wait()

    n_old = [norm[:, 0:128], norm[:, 128:256]]
    admit_bias = to_column(bias[0:1, :])
    forget_bias = to_column(bias[1:2, :])
    stabilizer = to_column(stab[...])
    q, keys, v, out_gate, forget, admit = [], [], [], [], [], []
    lane = lax.broadcasted_iota(jnp.int32, (24, 128), 1)
    row = lax.broadcasted_iota(jnp.int32, (24, 128), 0)

    def by_head(draft, first, width):
        return [flat[draft, pl.ds(first + i, 8, stride=width), :] for i in range(width)]

    def dot(a, b):
        total = a[0] * b[0]
        for i in range(1, len(a)):
            total = total + a[i] * b[i]
        return jnp.sum(total, axis=1, keepdims=True)

    for draft in range(2):
        wait_bytes(received.at[draft, pl.ds(0, 63)], sums_recv.at[draft])

        tails = None
        for half in range(2):
            for holder in range(4):
                sum_x = sum_y = None
                for lo in range(2):
                    for k in range(4):
                        one_x = received[draft, half * 32 + lo * 16 + k * 4 + holder].astype(F32)
                        one_y = received[draft, half * 32 + lo * 16 + holder * 4 + k].astype(F32)
                        sum_x = one_x if sum_x is None else sum_x + one_x
                        sum_y = one_y if sum_y is None else sum_y + one_y
                if half == 1:
                    tails = sum_x if tails is None else tails + sum_x
                for kind, total in enumerate((sum_x, sum_y)):
                    for side in range(2):
                        j = kind * 6 + side * 3
                        pair, last = total[j : j + 2], total[j + 2 : j + 3]
                        if half == 0 and side == 0:
                            pair = pair + total[12 + kind * 2 : 14 + kind * 2]
                        if half == 1 and side == 1 and kind == 1 and holder == 3:
                            last = last + total[12:13]
                        base = half * 48 + side * 24
                        tiles[pl.ds(base + kind * 8 + 2 * holder, 2), :] = pair
                        tiles[pl.ds(base + 16 + kind * 4 + holder, 1), :] = last

        tail_row = tails[13:14] + tails[14:15]
        for grp in range(4):
            block = tiles[pl.ds(grp * 24, 24), :]
            if grp:
                block = pltpu.roll(block, 4 * grp, 1)
            rolled[pl.ds(grp * 24 + 1, 24), :] = block
            if grp:
                before = rolled[pl.ds(grp * 24, 24), :]
                merged = jnp.where(lane >= 4 * grp, block, before)
                edge = (row == 0) & (lane >= 4 * grp - 4) & (lane < 4 * grp)
                block = jnp.where(edge, jnp.broadcast_to(tail_row, (24, 128)), merged)
            flat[draft, pl.ds(grp * 24, 24), :] = block
        gates = jnp.where(lane[0:1] >= 12, tail_row, rolled[pl.ds(96, 1), :])

        queries_t = flat[draft, 0:16, :].T
        for head in range(8):
            total = jnp.zeros((8, 512), F32)
            for part in range(8):
                block = memory[head, pl.ds(part * 32, 32), :]
                k = (part % 4) * 32
                at = head * 2 + part // 4
                product = queries_t[k : k + 32, at : at + 1] * block
                total = total + jnp.sum(product.reshape(4, 8, 512), axis=0)
            numer[pl.ds(head, 1), :] = jnp.sum(total, axis=0, keepdims=True)

        q.append(by_head(draft, 0, 2))
        keys.append([k * 0.0625 for k in by_head(draft, 16, 2)])
        v.append(by_head(draft, 32, 4))
        out_gate = by_head(draft, 64, 4)
        admit_pre = to_column(gates) + admit_bias
        forget_pre = to_column(gates, 8) + forget_bias
        log_forget = jnp.minimum(forget_pre, 0.0) - jnp.log1p(jnp.exp(-jnp.abs(forget_pre)))
        new_stabilizer = jnp.maximum(log_forget + stabilizer, admit_pre)
        forget.append(jnp.exp(log_forget + stabilizer - new_stabilizer))
        admit.append(jnp.exp(admit_pre - new_stabilizer))
        stabilizer = new_stabilizer

        on_old = forget[0] if draft == 0 else forget[0] * forget[1]
        on_keys = [admit[0]] if draft == 0 else [forget[1] * admit[0], admit[1]]
        on_values = [on_keys[i] * dot(q[draft], keys[i]) for i in range(draft + 1)]
        below = on_old * dot(q[draft], n_old)
        for part in on_values:
            below = below + part
        inverse = 1.0 / jnp.maximum(jnp.abs(below), 1.0)
        hidden = []
        for j in range(4):
            top = on_old * numer[:, pl.ds(j * 128, 128)]
            for i in range(draft + 1):
                top = top + on_values[i] * v[i][j]
            hidden.append(top * inverse)
        square_sum = hidden[0] * hidden[0]
        for j in range(1, 4):
            square_sum = square_sum + hidden[j] * hidden[j]
        mean = jnp.sum(jnp.sum(square_sum, axis=1, keepdims=True), axis=0, keepdims=True) * (1.0 / 4096.0)
        rescale = lax.rsqrt(mean + 1e-06)
        message = [
            hidden[j] * rescale * gain[pl.ds(j, 8, stride=4), :] * jax.nn.sigmoid(out_gate[j]) for j in range(4)
        ]
        readout[draft] = jnp.concatenate(message, axis=0).astype(BF16)
        for o_z, o_y, o_x in offsets(2):
            to = lax.rem(z_lo + o_z, 2) * 16 + lax.rem(y + o_y, 4) * 4 + lax.rem(x + o_x, 4)
            pltpu.make_async_remote_copy(
                src_ref=readout.at[draft], dst_ref=gathered.at[draft, loop_id],
                send_sem=gather_send.at[draft], recv_sem=gather_recv.at[draft],
                device_id=(to, grp_id), device_id_type=MESH,
            ).start()

    keep = pltpu.make_async_copy(readout, gathered.at[:, loop_id], own_sem)
    keep.start()

    for i in range(2):
        norm_out_ref[0, :, pl.ds(i * 128, 128)] = on_old * n_old[i] + on_keys[0] * keys[0][i] + on_keys[1] * keys[1][i]
    square = (8, 8)
    diagonal = lax.broadcasted_iota(jnp.int32, square, 0) == lax.broadcasted_iota(jnp.int32, square, 1)
    stab_out_ref[...] = jnp.sum(
        jnp.where(diagonal, jnp.broadcast_to(stabilizer, square), 0.0), axis=0, keepdims=True
    )

    for i in range(2):
        for j in range(4):
            scaled[i, :, pl.ds(j * 128, 128)] = on_keys[i] * v[i][j]
    keys_t = (jnp.concatenate([flat[0, 16:32, :], flat[1, 16:32, :]], axis=0) * 0.0625).T
    for head in range(8):
        fade = jnp.broadcast_to(on_old[head : head + 1, :], (32, 512))
        row0, row1 = scaled[0, pl.ds(head, 1), :], scaled[1, pl.ds(head, 1), :]
        for part in range(8):
            k = (part % 4) * 32
            at = head * 2 + part // 4
            k0 = keys_t[k : k + 32, at : at + 1]
            k1 = keys_t[k : k + 32, 16 + at : 17 + at]
            old = memory[head, pl.ds(part * 32, 32), :]
            memory_out_ref[0, head, pl.ds(part * 32, 32), :] = fade * old + k0 * row0 + k1 * row1

    keep.wait()
    for draft in range(2):
        wait_bytes(gathered.at[draft, pl.ds(0, 31)], gather_recv.at[draft])
        for block in range(4):
            piece = gathered[draft, pl.ds(block * 8, 8)].reshape(256, 128)
            gathered_f32[pl.ds(block * 256, 256), :] = piece.astype(F32)
        for j in range(4):
            for head in range(8):
                piece = gathered_f32[pl.ds(j * 8 + head, 32, stride=32), :]
                left[:, pl.ds((head * 4 + j) * 128, 128)] = piece.astype(BF16)
        product = jnp.dot(left[...], out_weight[...], preferred_element_type=F32)
        mixed_ref[draft] = product.astype(BF16)

    rows_copy.wait_send()
    tail_pair.wait_send()
    tail_all.wait_send()
    wait_bytes(weights.at[0, :, :, pl.ds(0, 384)], w_send)
    wait_bytes(weights.at[0], pass_send)
    wait_bytes(rows.at[pl.ds(0, 6)], ring_send)
    for draft in range(2):
        wait_bytes(send.at[draft, pl.ds(0, 63)], sums_send.at[draft])
        wait_bytes(gathered.at[draft, pl.ds(0, 31)], gather_send.at[draft])


def body(inputs, in_weight, gate_bias, memory, normalizer, stabilizer, out_gain, out_weight):
    vmem = pl.BlockSpec(memory_space=pltpu.VMEM)
    hbm = pl.BlockSpec(memory_space=pltpu.HBM)
    dma = pltpu.SemaphoreType.DMA
    out_shape = (
        jax.ShapeDtypeStruct((2, 32, 128), BF16),
        jax.ShapeDtypeStruct(memory.shape, F32),
        jax.ShapeDtypeStruct((1, 8, 256), F32),
        jax.ShapeDtypeStruct((1, 8), F32),
    )
    return pl.pallas_call(
        exchange_kernel,
        out_shape=out_shape,
        in_specs=[hbm] * 8,
        out_specs=(vmem,) * 4,
        scratch_shapes=[
            pltpu.VMEM((3076, 128), BF16),
            pltpu.VMEM((8, 256, 512), F32),
            pltpu.VMEM((4096, 128), BF16),
            pltpu.VMEM((2, 8), F32),
            pltpu.VMEM((8, 256), F32),
            pltpu.VMEM((1, 8), F32),
            pltpu.VMEM((32, 128), F32),
            pltpu.VMEM((2, 2, 32, 128), BF16),
            pltpu.VMEM((8, 2, 2, 32, 128), BF16),
            pltpu.VMEM((4, 16, 128), BF16),
            pltpu.VMEM((16, 128), F32),
            pltpu.VMEM((2, 2, 384, 512), BF16),
            pltpu.VMEM((1024, 128), F32),
            pltpu.VMEM((2, 64, 16, 128), BF16),
            pltpu.VMEM((2, 64, 16, 128), BF16),
            pltpu.VMEM((96, 128), F32),
            pltpu.VMEM((104, 128), F32),
            pltpu.VMEM((2, 96, 128), F32),
            pltpu.VMEM((8, 512), F32),
            pltpu.VMEM((2, 8, 512), F32),
            pltpu.VMEM((2, 32, 128), BF16),
            pltpu.VMEM((2, 32, 32, 128), BF16),
            pltpu.VMEM((1024, 128), F32),
            pltpu.VMEM((32, 4096), BF16),
            dma((8,)),
            dma,
            dma,
            dma,
            dma,
            dma,
            dma((2,)),
            dma((2,)),
            dma,
            dma((2, 4)),
            dma,
            dma,
            dma((2,)),
            dma((2,)),
            dma((2,)),
            dma((2,)),
            pltpu.SemaphoreType.REGULAR,
        ],
        compiler_params=pltpu.CompilerParams(
            collective_id=0, has_side_effects=True, vmem_limit_bytes=40 * 2**20
        ),
    )(*(
        pltpu.with_memory_space_constraint(operand, pltpu.HBM)
        for operand in (
            inputs, in_weight.T, gate_bias, memory, normalizer, stabilizer, out_gain.reshape(32, 128), out_weight
        )
    ))


def solution(mesh):
    in_specs = (
        P(None, "grp", "loop"),
        P("loop", "grp"),
        P(),
        P(("grp", "loop"), None, None, None),
        P(("grp", "loop"), None, None),
        P(("grp", "loop"), None),
        P(),
        P(None, "loop"),
    )
    out_specs = (
        P(None, "grp", "loop"),
        P(("grp", "loop"), None, None, None),
        P(("grp", "loop"), None, None),
        P(("grp", "loop"), None),
    )
    return jax.shard_map(body, mesh=mesh, in_specs=in_specs, out_specs=out_specs, check_vma=False)
```

```python
import jax
import jax.numpy as jnp
from jax import lax
from jax.experimental import pallas as pl
from jax.experimental.pallas import tpu as pltpu
from jax.sharding import PartitionSpec as P

MESH = pl.DeviceIdType.MESH
F32 = jnp.float32
BF16 = jnp.bfloat16


def split_low(value):
    return value - value.astype(BF16).astype(F32)


def offsets(deep):
    steps = [(o_z, o_y, o_x) for o_z in range(deep) for o_y in range(4) for o_x in range(4)]
    return sorted(steps[1:], key=lambda step: -sum(min(o, 4 - o) for o in step))


def to_column(row, shift=0):
    wide = jnp.broadcast_to(row, (8, row.shape[1]))
    lane = lax.broadcasted_iota(jnp.int32, wide.shape, 1)
    head = lax.broadcasted_iota(jnp.int32, wide.shape, 0)
    return jnp.sum(jnp.where(lane == head + shift, wide, 0.0), axis=1, keepdims=True)


def exchange_kernel(
    inputs_hbm, weight_hbm, bias_hbm, memory_hbm, norm_hbm, stab_hbm, gain_hbm, out_weight_hbm,
    mixed_ref, memory_out_ref, norm_out_ref, stab_out_ref,
    stage, memory, out_weight, bias, norm, stab, gain, rows_in, rows, tail, tail_f32, weights,
    send_f32, send, received, tiles, rolled, flat, numer, scaled, readout, gathered, gathered_f32, left,
    load_sem, own_sem, rows_send, rows_sem, ring_send, ring_sem, tail_send, tail_sem, w_send, w_sem, pass_send,
    pass_sem, sums_send, sums_recv, gather_send, gather_recv, ping_sem,
):
    loop_id = lax.axis_index("loop")
    grp_id = lax.axis_index("grp")
    x = lax.rem(loop_id, 4)
    y = lax.rem(lax.div(loop_id, 4), 4)
    z_lo = lax.div(loop_id, 16)
    z_hi = lax.div(grp_id, 2)
    core = lax.rem(grp_id, 2)

    def x_peer(o):
        return (z_lo * 16 + y * 4 + lax.rem(x + o, 4), grp_id)

    def y_peer(o):
        return (z_lo * 16 + lax.rem(y + o, 4) * 4 + x, grp_id)

    z_peer = (loop_id, (1 - z_hi) * 2 + core)
    other_lo = (1 - z_lo) * 16 + y * 4 + x
    z_near = [(other_lo, grp_id), (other_lo, (1 - z_hi) * 2 + core)]
    sibling = (loop_id, z_hi * 2 + 1 - core)

    loads = [
        pltpu.make_async_copy(src, dst, load_sem.at[i])
        for i, (src, dst) in enumerate((
            (inputs_hbm, rows_in.at[z_hi]),
            (weight_hbm, stage),
            (bias_hbm, bias),
            (stab_hbm, stab),
            (norm_hbm.at[0], norm),
            (gain_hbm, gain),
            (memory_hbm.at[0], memory),
            (out_weight_hbm, out_weight),
        ))
    ]
    for load in loads:
        load.start()

    barrier = pltpu.get_barrier_semaphore()
    peers = [x_peer(2), y_peer(2), z_peer] + z_near
    peers += [x_peer(1), x_peer(3), y_peer(1), y_peer(3), sibling]
    for peer in peers:
        pl.semaphore_signal(barrier, inc=1, device_id=peer, device_id_type=MESH)

    loads[0].wait()
    loads[1].wait()
    tail_f32[...] = jnp.zeros_like(tail_f32)
    tail_f32[0:4, :] = stage[3072:3076, :].astype(F32)
    tail[0] = pltpu.roll(tail_f32[...], grp_id * 4, 0).astype(BF16)

    pl.semaphore_wait(barrier, len(peers))

    def remote(src, dst, send_sem, recv_sem, peer):
        copy = pltpu.make_async_remote_copy(
            src_ref=src, dst_ref=dst, send_sem=send_sem, recv_sem=recv_sem, device_id=peer, device_id_type=MESH
        )
        copy.start()
        return copy

    def wait_bytes(ref, sem):
        pltpu.make_async_copy(ref, ref, sem).wait()

    rows_copy = remote(rows_in.at[z_hi], rows_in.at[z_hi], rows_send, rows_sem, z_peer)
    for peer in z_near:
        pl.semaphore_signal(ping_sem, inc=1, device_id=peer, device_id_type=MESH)
    tail_pair = remote(tail.at[0], tail.at[1], tail_send.at[0], tail_sem.at[0], sibling)

    def pieces(kind, holder, slot):
        wide = pl.ds(pl.multiple_of(kind * 1024 + holder * 256, 128), 256)
        one = pl.ds(pl.multiple_of(2048 + kind * 512 + holder * 128, 128), 128)
        deep = pl.ds(slot * 128, 128)
        return (
            (stage.at[wide], weights.at[kind, core, pl.ds(0, 256), deep]),
            (stage.at[one], weights.at[kind, core, pl.ds(256, 128), deep]),
        )

    for o in (2, 1, 3):
        for kind, coord, peer in ((0, x, x_peer(o)), (1, y, y_peer(o))):
            for src, dst in pieces(kind, lax.rem(coord + o, 4), 4 - o):
                remote(src, dst, w_send, w_sem.at[kind, 4 - o], peer)
    for kind, coord in ((0, x), (1, y)):
        for src, dst in pieces(kind, coord, 0):
            pltpu.make_async_copy(src, dst, own_sem).start()
            remote(src, dst, pass_send, pass_sem, sibling)

    tail_pair.wait_recv()
    tail[2] = tail[0] + tail[1]
    tail_all = remote(tail.at[2], tail.at[3], tail_send.at[1], tail_sem.at[1], z_peer)

    rows_copy.wait_recv()
    pl.semaphore_wait(ping_sem, 2)
    for o in (2, 1, 3):
        remote(rows_in, rows.at[4 - o], ring_send, ring_sem, x_peer(o))
        remote(rows_in, rows.at[8 - o], ring_send, ring_sem, y_peer(o))
    rows_own = rows_in[...].reshape(128, 128)
    tail_all.wait_recv()
    tail_columns = jnp.concatenate([tail[2] + tail[3], jnp.zeros((112, 128), BF16)], axis=0)
    across = (((1,), (1,)), ((), ()))
    tail_part = lax.dot_general(rows_own, tail_columns, across, preferred_element_type=F32)

    for slot in (3, 1, 2):
        for kind in range(2):
            block = weights.at[kind, core, :, pl.ds(slot * 128, 128)]
            wait_bytes(block, w_sem.at[kind, slot])
            remote(block, block, pass_send, pass_sem, sibling)
    wait_bytes(weights.at[0, 0, :, pl.ds(0, 256)], own_sem)
    wait_bytes(rows.at[pl.ds(0, 6)], ring_sem)
    wait_bytes(weights.at[0], pass_sem)

    parts = [
        [
            lax.dot_general(lhs, weights[kind, side], across, preferred_element_type=F32)
            for side in range(2)
        ]
        for kind in range(2)
        for lhs in [jnp.concatenate([rows_own] + [rows[kind * 4 + s].reshape(128, 128) for s in (1, 2, 3)], axis=1)]
    ]
    columns = [
        parts[kind][side][:, t * 128 : (t + 1) * 128] for kind in range(2) for side in range(2) for t in range(3)
    ]
    in_low = z_hi == 0
    columns += [
        jnp.where(in_low, split_low(columns[0]), split_low(columns[11])),
        jnp.where(in_low, split_low(columns[1]), tail_part),
        jnp.where(in_low, split_low(columns[6]), split_low(tail_part)),
        split_low(columns[7]),
    ]
    me = z_hi * 32 + loop_id
    for draft in range(2):
        for j, value in enumerate(columns):
            for half in range(2):
                first = half * 64 + draft * 32
                send_f32[pl.ds(half * 512 + j, 32, stride=16), :] = value[first : first + 32]
        for block in range(4):
            packed = send_f32[pl.ds(block * 256, 256), :].astype(BF16)
            send[draft, pl.ds(block * 16, 16)] = packed.reshape(16, 16, 128)
        for o_z, o_y, o_x in offsets(4):
            to = lax.rem(z_lo * 16 + z_hi * 32 + o_z * 16, 64) + lax.rem(y + o_y, 4) * 4 + lax.rem(x + o_x, 4)
            pltpu.make_async_remote_copy(
                src_ref=send.at[draft, to], dst_ref=received.at[draft, me],
                send_sem=sums_send.at[draft], recv_sem=sums_recv.at[draft],
                device_id=(lax.rem(to, 32), lax.div(to, 32) * 2 + core), device_id_type=MESH,
            ).start()
    keep = pltpu.make_async_copy(send.at[:, me], received.at[:, me], own_sem)
    keep.start()

    for load in loads[2:]:
        load.wait()
    keep.wait()

    n_old = [norm[:, 0:128], norm[:, 128:256]]
    admit_bias = to_column(bias[0:1, :])
    forget_bias = to_column(bias[1:2, :])
    stabilizer = to_column(stab[...])
    q, keys, v, out_gate, forget, admit = [], [], [], [], [], []
    lane = lax.broadcasted_iota(jnp.int32, (24, 128), 1)
    row = lax.broadcasted_iota(jnp.int32, (24, 128), 0)

    def by_head(draft, first, width):
        return [flat[draft, pl.ds(first + i, 8, stride=width), :] for i in range(width)]

    def dot(a, b):
        total = a[0] * b[0]
        for i in range(1, len(a)):
            total = total + a[i] * b[i]
        return jnp.sum(total, axis=1, keepdims=True)

    for draft in range(2):
        wait_bytes(received.at[draft, pl.ds(0, 63)], sums_recv.at[draft])

        tails = None
        for half in range(2):
            for holder in range(4):
                sum_x = sum_y = None
                for lo in range(2):
                    for k in range(4):
                        one_x = received[draft, half * 32 + lo * 16 + k * 4 + holder].astype(F32)
                        one_y = received[draft, half * 32 + lo * 16 + holder * 4 + k].astype(F32)
                        sum_x = one_x if sum_x is None else sum_x + one_x
                        sum_y = one_y if sum_y is None else sum_y + one_y
                if half == 1:
                    tails = sum_x if tails is None else tails + sum_x
                for kind, total in enumerate((sum_x, sum_y)):
                    for side in range(2):
                        j = kind * 6 + side * 3
                        pair, last = total[j : j + 2], total[j + 2 : j + 3]
                        if half == 0 and side == 0:
                            pair = pair + total[12 + kind * 2 : 14 + kind * 2]
                        if half == 1 and side == 1 and kind == 1 and holder == 3:
                            last = last + total[12:13]
                        base = half * 48 + side * 24
                        tiles[pl.ds(base + kind * 8 + 2 * holder, 2), :] = pair
                        tiles[pl.ds(base + 16 + kind * 4 + holder, 1), :] = last

        tail_row = tails[13:14] + tails[14:15]
        for grp in range(4):
            block = tiles[pl.ds(grp * 24, 24), :]
            if grp:
                block = pltpu.roll(block, 4 * grp, 1)
            rolled[pl.ds(grp * 24 + 1, 24), :] = block
            if grp:
                before = rolled[pl.ds(grp * 24, 24), :]
                merged = jnp.where(lane >= 4 * grp, block, before)
                edge = (row == 0) & (lane >= 4 * grp - 4) & (lane < 4 * grp)
                block = jnp.where(edge, jnp.broadcast_to(tail_row, (24, 128)), merged)
            flat[draft, pl.ds(grp * 24, 24), :] = block
        gates = jnp.where(lane[0:1] >= 12, tail_row, rolled[pl.ds(96, 1), :])

        queries_t = flat[draft, 0:16, :].T
        for head in range(8):
            total = jnp.zeros((8, 512), F32)
            for part in range(8):
                block = memory[head, pl.ds(part * 32, 32), :]
                k = (part % 4) * 32
                at = head * 2 + part // 4
                product = queries_t[k : k + 32, at : at + 1] * block
                total = total + jnp.sum(product.reshape(4, 8, 512), axis=0)
            numer[pl.ds(head, 1), :] = jnp.sum(total, axis=0, keepdims=True)

        q.append(by_head(draft, 0, 2))
        keys.append([k * 0.0625 for k in by_head(draft, 16, 2)])
        v.append(by_head(draft, 32, 4))
        out_gate = by_head(draft, 64, 4)
        admit_pre = to_column(gates) + admit_bias
        forget_pre = to_column(gates, 8) + forget_bias
        log_forget = jnp.minimum(forget_pre, 0.0) - jnp.log1p(jnp.exp(-jnp.abs(forget_pre)))
        new_stabilizer = jnp.maximum(log_forget + stabilizer, admit_pre)
        forget.append(jnp.exp(log_forget + stabilizer - new_stabilizer))
        admit.append(jnp.exp(admit_pre - new_stabilizer))
        stabilizer = new_stabilizer

        on_old = forget[0] if draft == 0 else forget[0] * forget[1]
        on_keys = [admit[0]] if draft == 0 else [forget[1] * admit[0], admit[1]]
        on_values = [on_keys[i] * dot(q[draft], keys[i]) for i in range(draft + 1)]
        below = on_old * dot(q[draft], n_old)
        for part in on_values:
            below = below + part
        inverse = 1.0 / jnp.maximum(jnp.abs(below), 1.0)
        hidden = []
        for j in range(4):
            top = on_old * numer[:, pl.ds(j * 128, 128)]
            for i in range(draft + 1):
                top = top + on_values[i] * v[i][j]
            hidden.append(top * inverse)
        square_sum = hidden[0] * hidden[0]
        for j in range(1, 4):
            square_sum = square_sum + hidden[j] * hidden[j]
        mean = jnp.sum(jnp.sum(square_sum, axis=1, keepdims=True), axis=0, keepdims=True) * (1.0 / 4096.0)
        rescale = lax.rsqrt(mean + 1e-06)
        message = [
            hidden[j] * rescale * gain[pl.ds(j, 8, stride=4), :] * jax.nn.sigmoid(out_gate[j]) for j in range(4)
        ]
        readout[draft] = jnp.concatenate(message, axis=0).astype(BF16)
        for o_z, o_y, o_x in offsets(2):
            to = lax.rem(z_lo + o_z, 2) * 16 + lax.rem(y + o_y, 4) * 4 + lax.rem(x + o_x, 4)
            pltpu.make_async_remote_copy(
                src_ref=readout.at[draft], dst_ref=gathered.at[draft, loop_id],
                send_sem=gather_send.at[draft], recv_sem=gather_recv.at[draft],
                device_id=(to, grp_id), device_id_type=MESH,
            ).start()

    keep = pltpu.make_async_copy(readout, gathered.at[:, loop_id], own_sem)
    keep.start()

    for i in range(2):
        norm_out_ref[0, :, pl.ds(i * 128, 128)] = on_old * n_old[i] + on_keys[0] * keys[0][i] + on_keys[1] * keys[1][i]
    square = (8, 8)
    diagonal = lax.broadcasted_iota(jnp.int32, square, 0) == lax.broadcasted_iota(jnp.int32, square, 1)
    stab_out_ref[...] = jnp.sum(
        jnp.where(diagonal, jnp.broadcast_to(stabilizer, square), 0.0), axis=0, keepdims=True
    )

    for i in range(2):
        for j in range(4):
            scaled[i, :, pl.ds(j * 128, 128)] = on_keys[i] * v[i][j]
    keys_t = (jnp.concatenate([flat[0, 16:32, :], flat[1, 16:32, :]], axis=0) * 0.0625).T
    for head in range(8):
        fade = jnp.broadcast_to(on_old[head : head + 1, :], (32, 512))
        row0, row1 = scaled[0, pl.ds(head, 1), :], scaled[1, pl.ds(head, 1), :]
        for part in range(8):
            k = (part % 4) * 32
            at = head * 2 + part // 4
            k0 = keys_t[k : k + 32, at : at + 1]
            k1 = keys_t[k : k + 32, 16 + at : 17 + at]
            old = memory[head, pl.ds(part * 32, 32), :]
            memory_out_ref[0, head, pl.ds(part * 32, 32), :] = fade * old + k0 * row0 + k1 * row1

    keep.wait()
    for draft in range(2):
        wait_bytes(gathered.at[draft, pl.ds(0, 31)], gather_recv.at[draft])
        for block in range(4):
            piece = gathered[draft, pl.ds(block * 8, 8)].reshape(256, 128)
            gathered_f32[pl.ds(block * 256, 256), :] = piece.astype(F32)
        for j in range(4):
            for head in range(8):
                piece = gathered_f32[pl.ds(j * 8 + head, 32, stride=32), :]
                left[:, pl.ds((head * 4 + j) * 128, 128)] = piece.astype(BF16)
        product = jnp.dot(left[...], out_weight[...], preferred_element_type=F32)
        mixed_ref[draft] = product.astype(BF16)

    rows_copy.wait_send()
    tail_pair.wait_send()
    tail_all.wait_send()
    wait_bytes(weights.at[0, :, :, pl.ds(0, 384)], w_send)
    wait_bytes(weights.at[0], pass_send)
    wait_bytes(rows.at[pl.ds(0, 6)], ring_send)
    for draft in range(2):
        wait_bytes(send.at[draft, pl.ds(0, 63)], sums_send.at[draft])
        wait_bytes(gathered.at[draft, pl.ds(0, 31)], gather_send.at[draft])


def hand_over_kernel(mixed, memory, norm, stab, mixed_out, memory_out, norm_out, stab_out, sem):
    pairs = [(memory.at[0, head], memory_out.at[0, head]) for head in range(8)]
    pairs += [(mixed, mixed_out), (norm, norm_out), (stab, stab_out)]
    copies = [pltpu.make_async_copy(src, dst, sem.at[i]) for i, (src, dst) in enumerate(pairs)]
    for copy in copies:
        copy.start()
    for copy in copies:
        copy.wait()


def body(inputs, in_weight, gate_bias, memory, normalizer, stabilizer, out_gain, out_weight):
    vmem = pl.BlockSpec(memory_space=pltpu.VMEM)
    hbm = pl.BlockSpec(memory_space=pltpu.HBM)
    dma = pltpu.SemaphoreType.DMA
    out_shape = (
        jax.ShapeDtypeStruct((2, 32, 128), BF16),
        jax.ShapeDtypeStruct(memory.shape, F32),
        jax.ShapeDtypeStruct((1, 8, 256), F32),
        jax.ShapeDtypeStruct((1, 8), F32),
    )
    results = pl.pallas_call(
        exchange_kernel,
        out_shape=out_shape,
        in_specs=[hbm] * 8,
        out_specs=(vmem,) * 4,
        scratch_shapes=[
            pltpu.VMEM((3076, 128), BF16),
            pltpu.VMEM((8, 256, 512), F32),
            pltpu.VMEM((4096, 128), BF16),
            pltpu.VMEM((2, 8), F32),
            pltpu.VMEM((8, 256), F32),
            pltpu.VMEM((1, 8), F32),
            pltpu.VMEM((32, 128), F32),
            pltpu.VMEM((2, 2, 32, 128), BF16),
            pltpu.VMEM((8, 2, 2, 32, 128), BF16),
            pltpu.VMEM((4, 16, 128), BF16),
            pltpu.VMEM((16, 128), F32),
            pltpu.VMEM((2, 2, 384, 512), BF16),
            pltpu.VMEM((1024, 128), F32),
            pltpu.VMEM((2, 64, 16, 128), BF16),
            pltpu.VMEM((2, 64, 16, 128), BF16),
            pltpu.VMEM((96, 128), F32),
            pltpu.VMEM((104, 128), F32),
            pltpu.VMEM((2, 96, 128), F32),
            pltpu.VMEM((8, 512), F32),
            pltpu.VMEM((2, 8, 512), F32),
            pltpu.VMEM((2, 32, 128), BF16),
            pltpu.VMEM((2, 32, 32, 128), BF16),
            pltpu.VMEM((1024, 128), F32),
            pltpu.VMEM((32, 4096), BF16),
            dma((8,)),
            dma,
            dma,
            dma,
            dma,
            dma,
            dma((2,)),
            dma((2,)),
            dma,
            dma((2, 4)),
            dma,
            dma,
            dma((2,)),
            dma((2,)),
            dma((2,)),
            dma((2,)),
            pltpu.SemaphoreType.REGULAR,
        ],
        compiler_params=pltpu.CompilerParams(
            collective_id=0, has_side_effects=True, vmem_limit_bytes=40 * 2**20
        ),
    )(*(
        pltpu.with_memory_space_constraint(operand, pltpu.HBM)
        for operand in (
            inputs, in_weight.T, gate_bias, memory, normalizer, stabilizer, out_gain.reshape(32, 128), out_weight
        )
    ))
    return pl.pallas_call(
        hand_over_kernel,
        out_shape=out_shape,
        in_specs=[vmem] * 4,
        out_specs=(hbm,) * 4,
        scratch_shapes=[dma((11,))],
        compiler_params=pltpu.CompilerParams(vmem_limit_bytes=2 * 2**20),
    )(*results)


def solution(mesh):
    in_specs = (
        P(None, "grp", "loop"),
        P("loop", "grp"),
        P(),
        P(("grp", "loop"), None, None, None),
        P(("grp", "loop"), None, None),
        P(("grp", "loop"), None),
        P(),
        P(None, "loop"),
    )
    out_specs = (
        P(None, "grp", "loop"),
        P(("grp", "loop"), None, None, None),
        P(("grp", "loop"), None, None),
        P(("grp", "loop"), None),
    )
    return jax.shard_map(body, mesh=mesh, in_specs=in_specs, out_specs=out_specs, check_vma=False)
```

```python
import jax
import jax.numpy as jnp
from jax import lax
from jax.experimental import pallas as pl
from jax.experimental.pallas import tpu as pltpu
from jax.sharding import PartitionSpec as P

MESH = pl.DeviceIdType.MESH
F32 = jnp.float32
BF16 = jnp.bfloat16


def split_low(value):
    return value - value.astype(BF16).astype(F32)


def offsets(deep):
    steps = [(o_z, o_y, o_x) for o_z in range(deep) for o_y in range(4) for o_x in range(4)]
    return sorted(steps[1:], key=lambda step: -sum(min(o, 4 - o) for o in step))


def to_column(row, shift=0):
    wide = jnp.broadcast_to(row, (8, row.shape[1]))
    lane = lax.broadcasted_iota(jnp.int32, wide.shape, 1)
    head = lax.broadcasted_iota(jnp.int32, wide.shape, 0)
    return jnp.sum(jnp.where(lane == head + shift, wide, 0.0), axis=1, keepdims=True)


def exchange_kernel(
    inputs_hbm, weight_hbm, bias_hbm, memory_hbm, norm_hbm, stab_hbm, gain_hbm, out_weight_hbm,
    mixed_ref, memory_out_ref, norm_out_ref, stab_out_ref,
    stage, memory, out_weight, bias, norm, stab, gain, rows_in, rows, tail, tail_f32, weights,
    send_f32, send, received, tiles, rolled, flat, numer, scaled, readout, gathered, gathered_f32, left,
    load_sem, own_sem, rows_send, rows_sem, ring_send, ring_sem, tail_send, tail_sem, w_send, w_sem, pass_send,
    pass_sem, sums_send, sums_recv, gather_send, gather_recv, ping_sem,
):
    loop_id = lax.axis_index("loop")
    grp_id = lax.axis_index("grp")
    x = lax.rem(loop_id, 4)
    y = lax.rem(lax.div(loop_id, 4), 4)
    z_lo = lax.div(loop_id, 16)
    z_hi = lax.div(grp_id, 2)
    core = lax.rem(grp_id, 2)

    def x_peer(o):
        return (z_lo * 16 + y * 4 + lax.rem(x + o, 4), grp_id)

    def y_peer(o):
        return (z_lo * 16 + lax.rem(y + o, 4) * 4 + x, grp_id)

    z_peer = (loop_id, (1 - z_hi) * 2 + core)
    other_lo = (1 - z_lo) * 16 + y * 4 + x
    z_near = [(other_lo, grp_id), (other_lo, (1 - z_hi) * 2 + core)]
    sibling = (loop_id, z_hi * 2 + 1 - core)

    barrier = pltpu.get_barrier_semaphore()
    peers = [x_peer(2), y_peer(2), z_peer] + z_near
    peers += [x_peer(1), x_peer(3), y_peer(1), y_peer(3), sibling]
    for peer in peers:
        pl.semaphore_signal(barrier, inc=1, device_id=peer, device_id_type=MESH)

    loads = [
        pltpu.make_async_copy(src, dst, load_sem.at[i])
        for i, (src, dst) in enumerate((
            (inputs_hbm, rows_in.at[z_hi]),
            (weight_hbm, stage),
            (bias_hbm, bias),
            (stab_hbm, stab),
            (norm_hbm.at[0], norm),
            (gain_hbm, gain),
            (memory_hbm.at[0], memory),
            (out_weight_hbm, out_weight),
        ))
    ]
    for load in loads:
        load.start()

    loads[0].wait()
    loads[1].wait()
    tail_f32[...] = jnp.zeros_like(tail_f32)
    tail_f32[0:4, :] = stage[3072:3076, :].astype(F32)
    tail[0] = pltpu.roll(tail_f32[...], grp_id * 4, 0).astype(BF16)

    pl.semaphore_wait(barrier, len(peers))

    def remote(src, dst, send_sem, recv_sem, peer):
        copy = pltpu.make_async_remote_copy(
            src_ref=src, dst_ref=dst, send_sem=send_sem, recv_sem=recv_sem, device_id=peer, device_id_type=MESH
        )
        copy.start()
        return copy

    def wait_bytes(ref, sem):
        pltpu.make_async_copy(ref, ref, sem).wait()

    rows_copy = remote(rows_in.at[z_hi], rows_in.at[z_hi], rows_send, rows_sem, z_peer)
    for peer in z_near:
        pl.semaphore_signal(ping_sem, inc=1, device_id=peer, device_id_type=MESH)
    tail_pair = remote(tail.at[0], tail.at[1], tail_send.at[0], tail_sem.at[0], sibling)

    def pieces(kind, holder, slot):
        wide = pl.ds(pl.multiple_of(kind * 1024 + holder * 256, 128), 256)
        one = pl.ds(pl.multiple_of(2048 + kind * 512 + holder * 128, 128), 128)
        deep = pl.ds(slot * 128, 128)
        return (
            (stage.at[wide], weights.at[kind, core, pl.ds(0, 256), deep]),
            (stage.at[one], weights.at[kind, core, pl.ds(256, 128), deep]),
        )

    for o in (2, 1, 3):
        for kind, coord, peer in ((0, x, x_peer(o)), (1, y, y_peer(o))):
            for src, dst in pieces(kind, lax.rem(coord + o, 4), 4 - o):
                remote(src, dst, w_send, w_sem.at[kind, 4 - o], peer)
    for kind, coord in ((0, x), (1, y)):
        for src, dst in pieces(kind, coord, 0):
            pltpu.make_async_copy(src, dst, own_sem).start()
            remote(src, dst, pass_send, pass_sem, sibling)

    tail_pair.wait_recv()
    tail[2] = tail[0] + tail[1]
    tail_all = remote(tail.at[2], tail.at[3], tail_send.at[1], tail_sem.at[1], z_peer)

    rows_copy.wait_recv()
    pl.semaphore_wait(ping_sem, 2)
    for o in (2, 1, 3):
        remote(rows_in, rows.at[4 - o], ring_send, ring_sem, x_peer(o))
        remote(rows_in, rows.at[8 - o], ring_send, ring_sem, y_peer(o))
    rows_own = rows_in[...].reshape(128, 128)
    tail_all.wait_recv()
    tail_columns = jnp.concatenate([tail[2] + tail[3], jnp.zeros((112, 128), BF16)], axis=0)
    across = (((1,), (1,)), ((), ()))
    tail_part = lax.dot_general(rows_own, tail_columns, across, preferred_element_type=F32)

    for slot in (3, 1, 2):
        for kind in range(2):
            block = weights.at[kind, core, :, pl.ds(slot * 128, 128)]
            wait_bytes(block, w_sem.at[kind, slot])
            remote(block, block, pass_send, pass_sem, sibling)
    wait_bytes(weights.at[0, 0, :, pl.ds(0, 256)], own_sem)
    wait_bytes(rows.at[pl.ds(0, 6)], ring_sem)
    wait_bytes(weights.at[0], pass_sem)

    parts = [
        lax.dot_general(lhs, weights[kind].reshape(768, 512), across, preferred_element_type=F32)
        for kind in range(2)
        for lhs in [jnp.concatenate([rows_own] + [rows[kind * 4 + s].reshape(128, 128) for s in (1, 2, 3)], axis=1)]
    ]
    columns = [
        parts[kind][:, t * 128 : (t + 1) * 128] for kind in range(2) for t in range(6)
    ]
    in_low = z_hi == 0
    columns += [
        jnp.where(in_low, split_low(columns[0]), split_low(columns[11])),
        jnp.where(in_low, split_low(columns[1]), tail_part),
        jnp.where(in_low, split_low(columns[6]), split_low(tail_part)),
        split_low(columns[7]),
    ]
    me = z_hi * 32 + loop_id
    for draft in range(2):
        for j, value in enumerate(columns):
            for half in range(2):
                first = half * 64 + draft * 32
                send_f32[pl.ds(half * 512 + j, 32, stride=16), :] = value[first : first + 32]
        for block in range(4):
            packed = send_f32[pl.ds(block * 256, 256), :].astype(BF16)
            send[draft, pl.ds(block * 16, 16)] = packed.reshape(16, 16, 128)

        def send_sums(to):
            pltpu.make_async_remote_copy(
                src_ref=send.at[draft, to], dst_ref=received.at[draft, me],
                send_sem=sums_send.at[draft], recv_sem=sums_recv.at[draft],
                device_id=(lax.rem(to, 32), lax.div(to, 32) * 2 + core), device_id_type=MESH,
            ).start()

        for half in range(2):
            for o_z, o_y, o_x in offsets(2):
                send_sums(half * 32 + lax.rem(z_lo + o_z, 2) * 16 + lax.rem(y + o_y, 4) * 4 + lax.rem(x + o_x, 4))

            @pl.when(z_hi != half)
            def _():
                send_sums(half * 32 + loop_id)

    keep = pltpu.make_async_copy(send.at[:, me], received.at[:, me], own_sem)
    keep.start()

    for load in loads[2:]:
        load.wait()
    keep.wait()

    n_old = [norm[:, 0:128], norm[:, 128:256]]
    admit_bias = to_column(bias[0:1, :])
    forget_bias = to_column(bias[1:2, :])
    stabilizer = to_column(stab[...])
    q, keys, v, out_gate, forget, admit = [], [], [], [], [], []
    lane = lax.broadcasted_iota(jnp.int32, (24, 128), 1)
    row = lax.broadcasted_iota(jnp.int32, (24, 128), 0)

    def by_head(draft, first, width):
        return [flat[draft, pl.ds(first + i, 8, stride=width), :] for i in range(width)]

    def dot(a, b):
        total = a[0] * b[0]
        for i in range(1, len(a)):
            total = total + a[i] * b[i]
        return jnp.sum(total, axis=1, keepdims=True)

    for draft in range(2):
        wait_bytes(received.at[draft, pl.ds(0, 63)], sums_recv.at[draft])

        tails = None
        for half in range(2):
            for holder in range(4):
                sum_x = sum_y = None
                for lo in range(2):
                    for k in range(4):
                        one_x = received[draft, half * 32 + lo * 16 + k * 4 + holder].astype(F32)
                        one_y = received[draft, half * 32 + lo * 16 + holder * 4 + k].astype(F32)
                        sum_x = one_x if sum_x is None else sum_x + one_x
                        sum_y = one_y if sum_y is None else sum_y + one_y
                if half == 1:
                    tails = sum_x if tails is None else tails + sum_x
                for kind, total in enumerate((sum_x, sum_y)):
                    for side in range(2):
                        j = kind * 6 + side * 3
                        pair, last = total[j : j + 2], total[j + 2 : j + 3]
                        if half == 0 and side == 0:
                            pair = pair + total[12 + kind * 2 : 14 + kind * 2]
                        if half == 1 and side == 1 and kind == 1 and holder == 3:
                            last = last + total[12:13]
                        base = half * 48 + side * 24
                        tiles[pl.ds(base + kind * 8 + 2 * holder, 2), :] = pair
                        tiles[pl.ds(base + 16 + kind * 4 + holder, 1), :] = last

        tail_row = tails[13:14] + tails[14:15]
        for grp in range(4):
            block = tiles[pl.ds(grp * 24, 24), :]
            if grp:
                block = pltpu.roll(block, 4 * grp, 1)
            rolled[pl.ds(grp * 24 + 1, 24), :] = block
            if grp:
                before = rolled[pl.ds(grp * 24, 24), :]
                merged = jnp.where(lane >= 4 * grp, block, before)
                edge = (row == 0) & (lane >= 4 * grp - 4) & (lane < 4 * grp)
                block = jnp.where(edge, jnp.broadcast_to(tail_row, (24, 128)), merged)
            flat[draft, pl.ds(grp * 24, 24), :] = block
        gates = jnp.where(lane[0:1] >= 12, tail_row, rolled[pl.ds(96, 1), :])

        queries_t = flat[draft, 0:16, :].T
        for head in range(8):
            total = jnp.zeros((8, 512), F32)
            for part in range(8):
                block = memory[head, pl.ds(part * 32, 32), :]
                k = (part % 4) * 32
                at = head * 2 + part // 4
                product = queries_t[k : k + 32, at : at + 1] * block
                total = total + jnp.sum(product.reshape(4, 8, 512), axis=0)
            numer[pl.ds(head, 1), :] = jnp.sum(total, axis=0, keepdims=True)

        q.append(by_head(draft, 0, 2))
        keys.append([k * 0.0625 for k in by_head(draft, 16, 2)])
        v.append(by_head(draft, 32, 4))
        out_gate = by_head(draft, 64, 4)
        admit_pre = to_column(gates) + admit_bias
        forget_pre = to_column(gates, 8) + forget_bias
        log_forget = jnp.minimum(forget_pre, 0.0) - jnp.log1p(jnp.exp(-jnp.abs(forget_pre)))
        new_stabilizer = jnp.maximum(log_forget + stabilizer, admit_pre)
        forget.append(jnp.exp(log_forget + stabilizer - new_stabilizer))
        admit.append(jnp.exp(admit_pre - new_stabilizer))
        stabilizer = new_stabilizer

        on_old = forget[0] if draft == 0 else forget[0] * forget[1]
        on_keys = [admit[0]] if draft == 0 else [forget[1] * admit[0], admit[1]]
        on_values = [on_keys[i] * dot(q[draft], keys[i]) for i in range(draft + 1)]
        below = on_old * dot(q[draft], n_old)
        for part in on_values:
            below = below + part
        inverse = 1.0 / jnp.maximum(jnp.abs(below), 1.0)
        hidden = []
        for j in range(4):
            top = on_old * numer[:, pl.ds(j * 128, 128)]
            for i in range(draft + 1):
                top = top + on_values[i] * v[i][j]
            hidden.append(top * inverse)
        square_sum = hidden[0] * hidden[0]
        for j in range(1, 4):
            square_sum = square_sum + hidden[j] * hidden[j]
        mean = jnp.sum(jnp.sum(square_sum, axis=1, keepdims=True), axis=0, keepdims=True) * (1.0 / 4096.0)
        rescale = lax.rsqrt(mean + 1e-06)
        message = [
            hidden[j] * rescale * gain[pl.ds(j, 8, stride=4), :] * jax.nn.sigmoid(out_gate[j]) for j in range(4)
        ]
        readout[draft] = jnp.concatenate(message, axis=0).astype(BF16)

        def send_readout(to):
            pltpu.make_async_remote_copy(
                src_ref=readout.at[draft], dst_ref=gathered.at[draft, loop_id],
                send_sem=gather_send.at[draft], recv_sem=gather_recv.at[draft],
                device_id=(to, grp_id), device_id_type=MESH,
            ).start()

        for to in sorted(range(32), key=lambda d: (min(d % 4, 4 - d % 4) + min(d // 4 % 4, 4 - d // 4 % 4) + d // 16)):
            @pl.when(loop_id != to)
            def _():
                send_readout(to)

    keep = pltpu.make_async_copy(readout, gathered.at[:, loop_id], own_sem)
    keep.start()

    for i in range(2):
        norm_out_ref[0, :, pl.ds(i * 128, 128)] = on_old * n_old[i] + on_keys[0] * keys[0][i] + on_keys[1] * keys[1][i]
    square = (8, 8)
    diagonal = lax.broadcasted_iota(jnp.int32, square, 0) == lax.broadcasted_iota(jnp.int32, square, 1)
    stab_out_ref[...] = jnp.sum(
        jnp.where(diagonal, jnp.broadcast_to(stabilizer, square), 0.0), axis=0, keepdims=True
    )

    for i in range(2):
        for j in range(4):
            scaled[i, :, pl.ds(j * 128, 128)] = on_keys[i] * v[i][j]
    keys_t = (jnp.concatenate([flat[0, 16:32, :], flat[1, 16:32, :]], axis=0) * 0.0625).T
    for head in range(8):
        fade = jnp.broadcast_to(on_old[head : head + 1, :], (32, 512))
        row0, row1 = scaled[0, pl.ds(head, 1), :], scaled[1, pl.ds(head, 1), :]
        for part in range(8):
            k = (part % 4) * 32
            at = head * 2 + part // 4
            k0 = keys_t[k : k + 32, at : at + 1]
            k1 = keys_t[k : k + 32, 16 + at : 17 + at]
            old = memory[head, pl.ds(part * 32, 32), :]
            memory_out_ref[0, head, pl.ds(part * 32, 32), :] = fade * old + k0 * row0 + k1 * row1

    keep.wait()
    for draft in range(2):
        wait_bytes(gathered.at[draft, pl.ds(0, 31)], gather_recv.at[draft])
        for block in range(4):
            piece = gathered[draft, pl.ds(block * 8, 8)].reshape(256, 128)
            gathered_f32[pl.ds(block * 256, 256), :] = piece.astype(F32)
        for j in range(4):
            for head in range(8):
                piece = gathered_f32[pl.ds(j * 8 + head, 32, stride=32), :]
                left[:, pl.ds((head * 4 + j) * 128, 128)] = piece.astype(BF16)
        product = jnp.dot(left[...], out_weight[...], preferred_element_type=F32)
        mixed_ref[draft] = product.astype(BF16)

    rows_copy.wait_send()
    tail_pair.wait_send()
    tail_all.wait_send()
    wait_bytes(weights.at[0, :, :, pl.ds(0, 384)], w_send)
    wait_bytes(weights.at[0], pass_send)
    wait_bytes(rows.at[pl.ds(0, 6)], ring_send)
    for draft in range(2):
        wait_bytes(send.at[draft, pl.ds(0, 63)], sums_send.at[draft])
        wait_bytes(gathered.at[draft, pl.ds(0, 31)], gather_send.at[draft])


def hand_over_kernel(mixed, memory, norm, stab, mixed_out, memory_out, norm_out, stab_out, sem):
    pairs = [(memory.at[0, head], memory_out.at[0, head]) for head in range(8)]
    pairs += [(mixed, mixed_out), (norm, norm_out), (stab, stab_out)]
    copies = [pltpu.make_async_copy(src, dst, sem.at[i]) for i, (src, dst) in enumerate(pairs)]
    for copy in copies:
        copy.start()
    for copy in copies:
        copy.wait()


def body(inputs, in_weight, gate_bias, memory, normalizer, stabilizer, out_gain, out_weight):
    vmem = pl.BlockSpec(memory_space=pltpu.VMEM)
    hbm = pl.BlockSpec(memory_space=pltpu.HBM)
    dma = pltpu.SemaphoreType.DMA
    out_shape = (
        jax.ShapeDtypeStruct((2, 32, 128), BF16),
        jax.ShapeDtypeStruct(memory.shape, F32),
        jax.ShapeDtypeStruct((1, 8, 256), F32),
        jax.ShapeDtypeStruct((1, 8), F32),
    )
    results = pl.pallas_call(
        exchange_kernel,
        out_shape=out_shape,
        in_specs=[hbm] * 8,
        out_specs=(vmem,) * 4,
        scratch_shapes=[
            pltpu.VMEM((3076, 128), BF16),
            pltpu.VMEM((8, 256, 512), F32),
            pltpu.VMEM((4096, 128), BF16),
            pltpu.VMEM((2, 8), F32),
            pltpu.VMEM((8, 256), F32),
            pltpu.VMEM((1, 8), F32),
            pltpu.VMEM((32, 128), F32),
            pltpu.VMEM((2, 2, 32, 128), BF16),
            pltpu.VMEM((8, 2, 2, 32, 128), BF16),
            pltpu.VMEM((4, 16, 128), BF16),
            pltpu.VMEM((16, 128), F32),
            pltpu.VMEM((2, 2, 384, 512), BF16),
            pltpu.VMEM((1024, 128), F32),
            pltpu.VMEM((2, 64, 16, 128), BF16),
            pltpu.VMEM((2, 64, 16, 128), BF16),
            pltpu.VMEM((96, 128), F32),
            pltpu.VMEM((104, 128), F32),
            pltpu.VMEM((2, 96, 128), F32),
            pltpu.VMEM((8, 512), F32),
            pltpu.VMEM((2, 8, 512), F32),
            pltpu.VMEM((2, 32, 128), BF16),
            pltpu.VMEM((2, 32, 32, 128), BF16),
            pltpu.VMEM((1024, 128), F32),
            pltpu.VMEM((32, 4096), BF16),
            dma((8,)),
            dma,
            dma,
            dma,
            dma,
            dma,
            dma((2,)),
            dma((2,)),
            dma,
            dma((2, 4)),
            dma,
            dma,
            dma((2,)),
            dma((2,)),
            dma((2,)),
            dma((2,)),
            pltpu.SemaphoreType.REGULAR,
        ],
        compiler_params=pltpu.CompilerParams(
            collective_id=0, has_side_effects=True, vmem_limit_bytes=40 * 2**20
        ),
    )(*(
        pltpu.with_memory_space_constraint(operand, pltpu.HBM)
        for operand in (
            inputs, in_weight.T, gate_bias, memory, normalizer, stabilizer, out_gain.reshape(32, 128), out_weight
        )
    ))
    return pl.pallas_call(
        hand_over_kernel,
        out_shape=out_shape,
        in_specs=[vmem] * 4,
        out_specs=(hbm,) * 4,
        scratch_shapes=[dma((11,))],
        compiler_params=pltpu.CompilerParams(vmem_limit_bytes=2 * 2**20),
    )(*results)


def solution(mesh):
    in_specs = (
        P(None, "grp", "loop"),
        P("loop", "grp"),
        P(),
        P(("grp", "loop"), None, None, None),
        P(("grp", "loop"), None, None),
        P(("grp", "loop"), None),
        P(),
        P(None, "loop"),
    )
    out_specs = (
        P(None, "grp", "loop"),
        P(("grp", "loop"), None, None, None),
        P(("grp", "loop"), None, None),
        P(("grp", "loop"), None),
    )
    return jax.shard_map(body, mesh=mesh, in_specs=in_specs, out_specs=out_specs, check_vma=False)
```

```python
import jax
import jax.numpy as jnp
from jax import lax
from jax.experimental import pallas as pl
from jax.experimental.pallas import tpu as pltpu
from jax.sharding import PartitionSpec as P

MESH = pl.DeviceIdType.MESH
F32 = jnp.float32
BF16 = jnp.bfloat16


def split_low(value):
    return value - value.astype(BF16).astype(F32)


def offsets(deep):
    steps = [(o_z, o_y, o_x) for o_z in range(deep) for o_y in range(4) for o_x in range(4)]
    return sorted(steps[1:], key=lambda step: -sum(min(o, 4 - o) for o in step))


def to_column(row, shift=0):
    wide = jnp.broadcast_to(row, (8, row.shape[1]))
    lane = lax.broadcasted_iota(jnp.int32, wide.shape, 1)
    head = lax.broadcasted_iota(jnp.int32, wide.shape, 0)
    return jnp.sum(jnp.where(lane == head + shift, wide, 0.0), axis=1, keepdims=True)


def exchange_kernel(
    inputs_hbm, weight_hbm, bias_hbm, memory_hbm, norm_hbm, stab_hbm, gain_hbm, out_weight_hbm,
    mixed_ref, memory_out_ref, norm_out_ref, stab_out_ref,
    stage, memory, out_weight, bias, norm, stab, gain, rows_in, rows, tail, tail_f32, weights,
    send_f32, send, received, tiles, rolled, flat, numer, scaled, readout, gathered, gathered_f32, left,
    load_sem, own_sem, rows_send, rows_sem, ring_send, ring_sem, tail_send, tail_sem, w_send, w_sem, pass_send,
    pass_sem, sums_send, sums_recv, gather_send, gather_recv, ping_sem,
):
    loop_id = lax.axis_index("loop")
    grp_id = lax.axis_index("grp")
    x = lax.rem(loop_id, 4)
    y = lax.rem(lax.div(loop_id, 4), 4)
    z_lo = lax.div(loop_id, 16)
    z_hi = lax.div(grp_id, 2)
    core = lax.rem(grp_id, 2)

    def x_peer(o):
        return (z_lo * 16 + y * 4 + lax.rem(x + o, 4), grp_id)

    def y_peer(o):
        return (z_lo * 16 + lax.rem(y + o, 4) * 4 + x, grp_id)

    z_peer = (loop_id, (1 - z_hi) * 2 + core)
    other_lo = (1 - z_lo) * 16 + y * 4 + x
    z_near = [(other_lo, grp_id), (other_lo, (1 - z_hi) * 2 + core)]
    sibling = (loop_id, z_hi * 2 + 1 - core)

    barrier = pltpu.get_barrier_semaphore()
    peers = [x_peer(2), y_peer(2), z_peer] + z_near
    peers += [x_peer(1), x_peer(3), y_peer(1), y_peer(3), sibling]
    for peer in peers:
        pl.semaphore_signal(barrier, inc=1, device_id=peer, device_id_type=MESH)

    loads = [
        pltpu.make_async_copy(src, dst, load_sem.at[i])
        for i, (src, dst) in enumerate((
            (inputs_hbm, rows_in.at[z_hi]),
            (weight_hbm, stage),
            (bias_hbm, bias),
            (stab_hbm, stab),
            (norm_hbm.at[0], norm),
            (gain_hbm, gain),
            (memory_hbm.at[0], memory),
            (out_weight_hbm, out_weight),
        ))
    ]
    for load in loads:
        load.start()

    loads[0].wait()
    loads[1].wait()
    tail_f32[...] = jnp.zeros_like(tail_f32)
    tail_f32[0:4, :] = stage[3072:3076, :].astype(F32)
    tail[0] = pltpu.roll(tail_f32[...], grp_id * 4, 0).astype(BF16)

    pl.semaphore_wait(barrier, len(peers))

    def remote(src, dst, send_sem, recv_sem, peer):
        copy = pltpu.make_async_remote_copy(
            src_ref=src, dst_ref=dst, send_sem=send_sem, recv_sem=recv_sem, device_id=peer, device_id_type=MESH
        )
        copy.start()
        return copy

    def wait_bytes(ref, sem):
        pltpu.make_async_copy(ref, ref, sem).wait()

    rows_copy = remote(rows_in.at[z_hi], rows_in.at[z_hi], rows_send, rows_sem, z_peer)
    for peer in z_near:
        pl.semaphore_signal(ping_sem, inc=1, device_id=peer, device_id_type=MESH)
    tail_pair = remote(tail.at[0], tail.at[1], tail_send.at[0], tail_sem.at[0], sibling)

    def landing(which, kind, slot):
        tiles_at = pl.ds(0, 256) if which == 0 else pl.ds(256, 128)
        return weights.at[kind, core, tiles_at, pl.ds(slot * 128, 128)]

    def piece(which, kind, holder):
        if which == 0:
            return stage.at[pl.ds(pl.multiple_of(kind * 1024 + holder * 256, 128), 256)]
        return stage.at[pl.ds(pl.multiple_of(2048 + kind * 512 + holder * 128, 128), 128)]

    def send_pieces(which, steps):
        for o in steps:
            for kind, coord, peer in ((0, x, x_peer(o)), (1, y, y_peer(o))):
                src = piece(which, kind, lax.rem(coord + o, 4))
                remote(src, landing(which, kind, 4 - o), w_send, w_sem.at[kind, 4 - o, which], peer)

    send_pieces(0, (2, 1, 3))
    send_pieces(1, (2, 1, 3))
    for o in (2, 1, 3):
        remote(rows_in.at[z_hi], rows.at[4 - o, z_hi], ring_send.at[0], ring_sem.at[0], x_peer(o))
        remote(rows_in.at[z_hi], rows.at[8 - o, z_hi], ring_send.at[0], ring_sem.at[0], y_peer(o))
    for which in range(2):
        for kind, coord in ((0, x), (1, y)):
            src, dst = piece(which, kind, coord), landing(which, kind, 0)
            pltpu.make_async_copy(src, dst, own_sem).start()
            remote(src, dst, pass_send, pass_sem.at[which], sibling)

    tail_pair.wait_recv()
    tail[2] = tail[0] + tail[1]
    tail_all = remote(tail.at[2], tail.at[3], tail_send.at[1], tail_sem.at[1], z_peer)

    rows_copy.wait_recv()
    pl.semaphore_wait(ping_sem, 2)
    for o in (2, 1, 3):
        remote(rows_in.at[1 - z_hi], rows.at[4 - o, 1 - z_hi], ring_send.at[1], ring_sem.at[1], x_peer(o))
        remote(rows_in.at[1 - z_hi], rows.at[8 - o, 1 - z_hi], ring_send.at[1], ring_sem.at[1], y_peer(o))
    rows_own = rows_in[...].reshape(128, 128)

    for which in range(2):
        for slot in (3, 1, 2):
            for kind in range(2):
                block = landing(which, kind, slot)
                wait_bytes(block, w_sem.at[kind, slot, which])
                remote(block, block, pass_send, pass_sem.at[which], sibling)
    tail_all.wait_recv()
    tail_columns = jnp.concatenate([tail[2] + tail[3], jnp.zeros((112, 128), BF16)], axis=0)
    across = (((1,), (1,)), ((), ()))
    tail_part = lax.dot_general(rows_own, tail_columns, across, preferred_element_type=F32)
    wait_bytes(weights.at[0, 0, :, pl.ds(0, 256)], own_sem)
    for half in range(2):
        wait_bytes(rows.at[pl.ds(0, 3)], ring_sem.at[half])

    def put(j, value):
        for draft in range(2):
            for half in range(2):
                first = half * 64 + draft * 32
                send_f32[draft, pl.ds(half * 512 + j, 32, stride=16), :] = value[first : first + 32]

    in_low = z_hi == 0
    wait_bytes(weights.at[0, :, pl.ds(0, 256)], pass_sem.at[0])
    lefts, lows = [], []
    for kind in range(2):
        lhs = jnp.concatenate([rows_own] + [rows[kind * 4 + s].reshape(128, 128) for s in (1, 2, 3)], axis=1)
        lefts.append(lhs)
        part = lax.dot_general(
            lhs, weights[kind, :, 0:256, :].reshape(512, 512), across, preferred_element_type=F32
        )
        for side in range(2):
            for t in range(2):
                column = part[:, side * 256 + t * 128 : side * 256 + (t + 1) * 128]
                put(kind * 6 + side * 3 + t, column)
                if side == 0:
                    lows.append(split_low(column))
    put(13, jnp.where(in_low, lows[1], tail_part))
    put(14, jnp.where(in_low, lows[2], split_low(tail_part)))
    put(15, lows[3])
    wait_bytes(weights.at[0, :, pl.ds(256, 128)], pass_sem.at[1])
    for kind in range(2):
        part = lax.dot_general(
            lefts[kind], weights[kind, :, 256:384, :].reshape(256, 512), across, preferred_element_type=F32
        )
        for side in range(2):
            column = part[:, side * 128 : (side + 1) * 128]
            put(kind * 6 + side * 3 + 2, column)
    put(12, jnp.where(in_low, lows[0], split_low(column)))
    me = z_hi * 32 + loop_id
    for draft in range(2):
        for block in range(4):
            packed = send_f32[draft, pl.ds(block * 256, 256), :].astype(BF16)
            send[draft, pl.ds(block * 16, 16)] = packed.reshape(16, 16, 128)

        def send_sums(to):
            pltpu.make_async_remote_copy(
                src_ref=send.at[draft, to], dst_ref=received.at[draft, me],
                send_sem=sums_send.at[draft], recv_sem=sums_recv.at[draft],
                device_id=(lax.rem(to, 32), lax.div(to, 32) * 2 + core), device_id_type=MESH,
            ).start()

        for half in range(2):
            for o_z, o_y, o_x in offsets(2):
                send_sums(half * 32 + lax.rem(z_lo + o_z, 2) * 16 + lax.rem(y + o_y, 4) * 4 + lax.rem(x + o_x, 4))

            @pl.when(z_hi != half)
            def _():
                send_sums(half * 32 + loop_id)

    keep = pltpu.make_async_copy(send.at[:, me], received.at[:, me], own_sem)
    keep.start()

    for load in loads[2:]:
        load.wait()
    keep.wait()

    n_old = [norm[:, 0:128], norm[:, 128:256]]
    admit_bias = to_column(bias[0:1, :])
    forget_bias = to_column(bias[1:2, :])
    stabilizer = to_column(stab[...])
    q, keys, v, out_gate, forget, admit = [], [], [], [], [], []
    lane = lax.broadcasted_iota(jnp.int32, (24, 128), 1)
    row = lax.broadcasted_iota(jnp.int32, (24, 128), 0)

    def by_head(draft, first, width):
        return [flat[draft, pl.ds(first + i, 8, stride=width), :] for i in range(width)]

    def dot(a, b):
        total = a[0] * b[0]
        for i in range(1, len(a)):
            total = total + a[i] * b[i]
        return jnp.sum(total, axis=1, keepdims=True)

    for draft in range(2):
        wait_bytes(received.at[draft, pl.ds(0, 63)], sums_recv.at[draft])

        tails = None
        for half in range(2):
            for holder in range(4):
                sum_x = sum_y = None
                for lo in range(2):
                    for k in range(4):
                        one_x = received[draft, half * 32 + lo * 16 + k * 4 + holder].astype(F32)
                        one_y = received[draft, half * 32 + lo * 16 + holder * 4 + k].astype(F32)
                        sum_x = one_x if sum_x is None else sum_x + one_x
                        sum_y = one_y if sum_y is None else sum_y + one_y
                if half == 1:
                    tails = sum_x if tails is None else tails + sum_x
                for kind, total in enumerate((sum_x, sum_y)):
                    for side in range(2):
                        j = kind * 6 + side * 3
                        pair, last = total[j : j + 2], total[j + 2 : j + 3]
                        if half == 0 and side == 0:
                            pair = pair + total[12 + kind * 2 : 14 + kind * 2]
                        if half == 1 and side == 1 and kind == 1 and holder == 3:
                            last = last + total[12:13]
                        base = half * 48 + side * 24
                        tiles[pl.ds(base + kind * 8 + 2 * holder, 2), :] = pair
                        tiles[pl.ds(base + 16 + kind * 4 + holder, 1), :] = last

        tail_row = tails[13:14] + tails[14:15]
        for grp in range(4):
            block = tiles[pl.ds(grp * 24, 24), :]
            if grp:
                block = pltpu.roll(block, 4 * grp, 1)
            rolled[pl.ds(grp * 24 + 1, 24), :] = block
            if grp:
                before = rolled[pl.ds(grp * 24, 24), :]
                merged = jnp.where(lane >= 4 * grp, block, before)
                edge = (row == 0) & (lane >= 4 * grp - 4) & (lane < 4 * grp)
                block = jnp.where(edge, jnp.broadcast_to(tail_row, (24, 128)), merged)
            flat[draft, pl.ds(grp * 24, 24), :] = block
        gates = jnp.where(lane[0:1] >= 12, tail_row, rolled[pl.ds(96, 1), :])

        queries_t = flat[draft, 0:16, :].T
        for head in range(8):
            total = jnp.zeros((8, 512), F32)
            for part in range(8):
                block = memory[head, pl.ds(part * 32, 32), :]
                k = (part % 4) * 32
                at = head * 2 + part // 4
                product = queries_t[k : k + 32, at : at + 1] * block
                total = total + jnp.sum(product.reshape(4, 8, 512), axis=0)
            numer[pl.ds(head, 1), :] = jnp.sum(total, axis=0, keepdims=True)

        q.append(by_head(draft, 0, 2))
        keys.append([k * 0.0625 for k in by_head(draft, 16, 2)])
        v.append(by_head(draft, 32, 4))
        out_gate = by_head(draft, 64, 4)
        admit_pre = to_column(gates) + admit_bias
        forget_pre = to_column(gates, 8) + forget_bias
        log_forget = jnp.minimum(forget_pre, 0.0) - jnp.log1p(jnp.exp(-jnp.abs(forget_pre)))
        new_stabilizer = jnp.maximum(log_forget + stabilizer, admit_pre)
        forget.append(jnp.exp(log_forget + stabilizer - new_stabilizer))
        admit.append(jnp.exp(admit_pre - new_stabilizer))
        stabilizer = new_stabilizer

        on_old = forget[0] if draft == 0 else forget[0] * forget[1]
        on_keys = [admit[0]] if draft == 0 else [forget[1] * admit[0], admit[1]]
        on_values = [on_keys[i] * dot(q[draft], keys[i]) for i in range(draft + 1)]
        below = on_old * dot(q[draft], n_old)
        for part in on_values:
            below = below + part
        inverse = 1.0 / jnp.maximum(jnp.abs(below), 1.0)
        hidden = []
        for j in range(4):
            top = on_old * numer[:, pl.ds(j * 128, 128)]
            for i in range(draft + 1):
                top = top + on_values[i] * v[i][j]
            hidden.append(top * inverse)
        square_sum = hidden[0] * hidden[0]
        for j in range(1, 4):
            square_sum = square_sum + hidden[j] * hidden[j]
        mean = jnp.sum(jnp.sum(square_sum, axis=1, keepdims=True), axis=0, keepdims=True) * (1.0 / 4096.0)
        rescale = lax.rsqrt(mean + 1e-06)
        message = [
            hidden[j] * rescale * gain[pl.ds(j, 8, stride=4), :] * jax.nn.sigmoid(out_gate[j]) for j in range(4)
        ]
        readout[draft] = jnp.concatenate(message, axis=0).astype(BF16)

        def send_readout(to):
            pltpu.make_async_remote_copy(
                src_ref=readout.at[draft], dst_ref=gathered.at[draft, loop_id],
                send_sem=gather_send.at[draft], recv_sem=gather_recv.at[draft],
                device_id=(to, grp_id), device_id_type=MESH,
            ).start()

        for to in sorted(range(32), key=lambda d: (min(d % 4, 4 - d % 4) + min(d // 4 % 4, 4 - d // 4 % 4) + d // 16)):
            @pl.when(loop_id != to)
            def _():
                send_readout(to)

    keep = pltpu.make_async_copy(readout, gathered.at[:, loop_id], own_sem)
    keep.start()

    for i in range(2):
        norm_out_ref[0, :, pl.ds(i * 128, 128)] = on_old * n_old[i] + on_keys[0] * keys[0][i] + on_keys[1] * keys[1][i]
    square = (8, 8)
    diagonal = lax.broadcasted_iota(jnp.int32, square, 0) == lax.broadcasted_iota(jnp.int32, square, 1)
    stab_out_ref[...] = jnp.sum(
        jnp.where(diagonal, jnp.broadcast_to(stabilizer, square), 0.0), axis=0, keepdims=True
    )

    for i in range(2):
        for j in range(4):
            scaled[i, :, pl.ds(j * 128, 128)] = on_keys[i] * v[i][j]
    keys_t = (jnp.concatenate([flat[0, 16:32, :], flat[1, 16:32, :]], axis=0) * 0.0625).T
    for head in range(8):
        fade = jnp.broadcast_to(on_old[head : head + 1, :], (32, 512))
        row0, row1 = scaled[0, pl.ds(head, 1), :], scaled[1, pl.ds(head, 1), :]
        for part in range(8):
            k = (part % 4) * 32
            at = head * 2 + part // 4
            k0 = keys_t[k : k + 32, at : at + 1]
            k1 = keys_t[k : k + 32, 16 + at : 17 + at]
            old = memory[head, pl.ds(part * 32, 32), :]
            memory_out_ref[0, head, pl.ds(part * 32, 32), :] = fade * old + k0 * row0 + k1 * row1

    keep.wait()
    for draft in range(2):
        wait_bytes(gathered.at[draft, pl.ds(0, 31)], gather_recv.at[draft])
        for block in range(4):
            piece = gathered[draft, pl.ds(block * 8, 8)].reshape(256, 128)
            gathered_f32[pl.ds(block * 256, 256), :] = piece.astype(F32)
        for j in range(4):
            for head in range(8):
                piece = gathered_f32[pl.ds(j * 8 + head, 32, stride=32), :]
                left[:, pl.ds((head * 4 + j) * 128, 128)] = piece.astype(BF16)
        product = jnp.dot(left[...], out_weight[...], preferred_element_type=F32)
        mixed_ref[draft] = product.astype(BF16)

    rows_copy.wait_send()
    tail_pair.wait_send()
    tail_all.wait_send()
    wait_bytes(weights.at[0, :, :, pl.ds(0, 384)], w_send)
    wait_bytes(weights.at[0], pass_send)
    for half in range(2):
        wait_bytes(rows.at[pl.ds(0, 3)], ring_send.at[half])
    for draft in range(2):
        wait_bytes(send.at[draft, pl.ds(0, 63)], sums_send.at[draft])
        wait_bytes(gathered.at[draft, pl.ds(0, 31)], gather_send.at[draft])


def hand_over_kernel(mixed, memory, norm, stab, mixed_out, memory_out, norm_out, stab_out, sem):
    pairs = [(memory.at[0, head], memory_out.at[0, head]) for head in range(8)]
    pairs += [(mixed, mixed_out), (norm, norm_out), (stab, stab_out)]
    copies = [pltpu.make_async_copy(src, dst, sem.at[i]) for i, (src, dst) in enumerate(pairs)]
    for copy in copies:
        copy.start()
    for copy in copies:
        copy.wait()


def body(inputs, in_weight, gate_bias, memory, normalizer, stabilizer, out_gain, out_weight):
    vmem = pl.BlockSpec(memory_space=pltpu.VMEM)
    hbm = pl.BlockSpec(memory_space=pltpu.HBM)
    dma = pltpu.SemaphoreType.DMA
    out_shape = (
        jax.ShapeDtypeStruct((2, 32, 128), BF16),
        jax.ShapeDtypeStruct(memory.shape, F32),
        jax.ShapeDtypeStruct((1, 8, 256), F32),
        jax.ShapeDtypeStruct((1, 8), F32),
    )
    results = pl.pallas_call(
        exchange_kernel,
        out_shape=out_shape,
        in_specs=[hbm] * 8,
        out_specs=(vmem,) * 4,
        scratch_shapes=[
            pltpu.VMEM((3076, 128), BF16),
            pltpu.VMEM((8, 256, 512), F32),
            pltpu.VMEM((4096, 128), BF16),
            pltpu.VMEM((2, 8), F32),
            pltpu.VMEM((8, 256), F32),
            pltpu.VMEM((1, 8), F32),
            pltpu.VMEM((32, 128), F32),
            pltpu.VMEM((2, 2, 32, 128), BF16),
            pltpu.VMEM((8, 2, 2, 32, 128), BF16),
            pltpu.VMEM((4, 16, 128), BF16),
            pltpu.VMEM((16, 128), F32),
            pltpu.VMEM((2, 2, 384, 512), BF16),
            pltpu.VMEM((2, 1024, 128), F32),
            pltpu.VMEM((2, 64, 16, 128), BF16),
            pltpu.VMEM((2, 64, 16, 128), BF16),
            pltpu.VMEM((96, 128), F32),
            pltpu.VMEM((104, 128), F32),
            pltpu.VMEM((2, 96, 128), F32),
            pltpu.VMEM((8, 512), F32),
            pltpu.VMEM((2, 8, 512), F32),
            pltpu.VMEM((2, 32, 128), BF16),
            pltpu.VMEM((2, 32, 32, 128), BF16),
            pltpu.VMEM((1024, 128), F32),
            pltpu.VMEM((32, 4096), BF16),
            dma((8,)),
            dma,
            dma,
            dma,
            dma((2,)),
            dma((2,)),
            dma((2,)),
            dma((2,)),
            dma,
            dma((2, 4, 2)),
            dma,
            dma((2,)),
            dma((2,)),
            dma((2,)),
            dma((2,)),
            dma((2,)),
            pltpu.SemaphoreType.REGULAR,
        ],
        compiler_params=pltpu.CompilerParams(
            collective_id=0, has_side_effects=True, vmem_limit_bytes=40 * 2**20
        ),
    )(*(
        pltpu.with_memory_space_constraint(operand, pltpu.HBM)
        for operand in (
            inputs, in_weight.T, gate_bias, memory, normalizer, stabilizer, out_gain.reshape(32, 128), out_weight
        )
    ))
    return pl.pallas_call(
        hand_over_kernel,
        out_shape=out_shape,
        in_specs=[vmem] * 4,
        out_specs=(hbm,) * 4,
        scratch_shapes=[dma((11,))],
        compiler_params=pltpu.CompilerParams(vmem_limit_bytes=2 * 2**20),
    )(*results)


def solution(mesh):
    in_specs = (
        P(None, "grp", "loop"),
        P("loop", "grp"),
        P(),
        P(("grp", "loop"), None, None, None),
        P(("grp", "loop"), None, None),
        P(("grp", "loop"), None),
        P(),
        P(None, "loop"),
    )
    out_specs = (
        P(None, "grp", "loop"),
        P(("grp", "loop"), None, None, None),
        P(("grp", "loop"), None, None),
        P(("grp", "loop"), None),
    )
    return jax.shard_map(body, mesh=mesh, in_specs=in_specs, out_specs=out_specs, check_vma=False)
```

```python
import jax
import jax.numpy as jnp
from jax import lax
from jax.experimental import pallas as pl
from jax.experimental.pallas import tpu as pltpu
from jax.sharding import PartitionSpec as P

MESH = pl.DeviceIdType.MESH
F32 = jnp.float32
BF16 = jnp.bfloat16


def split_low(value):
    return value - value.astype(BF16).astype(F32)


def offsets(deep):
    steps = [(o_z, o_y, o_x) for o_z in range(deep) for o_y in range(4) for o_x in range(4)]
    return sorted(steps[1:], key=lambda step: -sum(min(o, 4 - o) for o in step))


def to_column(row, shift=0):
    wide = jnp.broadcast_to(row, (8, row.shape[1]))
    lane = lax.broadcasted_iota(jnp.int32, wide.shape, 1)
    head = lax.broadcasted_iota(jnp.int32, wide.shape, 0)
    return jnp.sum(jnp.where(lane == head + shift, wide, 0.0), axis=1, keepdims=True)


def exchange_kernel(
    inputs_hbm, weight_hbm, bias_hbm, memory_hbm, norm_hbm, stab_hbm, gain_hbm, out_weight_hbm,
    mixed_ref, memory_out_ref, norm_out_ref, stab_out_ref,
    stage, memory, out_weight, bias, norm, stab, gain, rows_in, rows, tail, tail_f32, weights,
    send_f32, send, received, tiles, rolled, flat, numer, scaled, readout, gathered, gathered_f32, left,
    load_sem, own_sem, rows_send, rows_sem, ring_send, ring_sem, tail_send, tail_sem, w_send, w_sem, pass_send,
    pass_sem, sums_send, sums_recv, gather_send, gather_recv, ping_sem,
):
    loop_id = lax.axis_index("loop")
    grp_id = lax.axis_index("grp")
    x = lax.rem(loop_id, 4)
    y = lax.rem(lax.div(loop_id, 4), 4)
    z_lo = lax.div(loop_id, 16)
    z_hi = lax.div(grp_id, 2)
    core = lax.rem(grp_id, 2)

    def x_peer(o):
        return (z_lo * 16 + y * 4 + lax.rem(x + o, 4), grp_id)

    def y_peer(o):
        return (z_lo * 16 + lax.rem(y + o, 4) * 4 + x, grp_id)

    z_peer = (loop_id, (1 - z_hi) * 2 + core)
    other_lo = (1 - z_lo) * 16 + y * 4 + x
    z_near = [(other_lo, grp_id), (other_lo, (1 - z_hi) * 2 + core)]
    sibling = (loop_id, z_hi * 2 + 1 - core)

    barrier = pltpu.get_barrier_semaphore()
    peers = [x_peer(2), y_peer(2), z_peer] + z_near
    peers += [x_peer(1), x_peer(3), y_peer(1), y_peer(3), sibling]
    for peer in peers:
        pl.semaphore_signal(barrier, inc=1, device_id=peer, device_id_type=MESH)

    loads = [
        pltpu.make_async_copy(src, dst, load_sem.at[i])
        for i, (src, dst) in enumerate((
            (inputs_hbm, rows_in.at[z_hi]),
            (weight_hbm, stage),
            (bias_hbm, bias),
            (stab_hbm, stab),
            (norm_hbm.at[0], norm),
            (gain_hbm, gain.at[pl.ds(0, 32)]),
            (memory_hbm.at[0], memory),
            (out_weight_hbm, out_weight),
        ))
    ]
    for load in loads:
        load.start()

    loads[0].wait()
    loads[1].wait()
    tail_f32[...] = jnp.zeros_like(tail_f32)
    tail_f32[0:4, :] = stage[3072:3076, :].astype(F32)
    tail[0] = pltpu.roll(tail_f32[...], grp_id * 4, 0).astype(BF16)

    pl.semaphore_wait(barrier, len(peers))

    def remote(src, dst, send_sem, recv_sem, peer):
        copy = pltpu.make_async_remote_copy(
            src_ref=src, dst_ref=dst, send_sem=send_sem, recv_sem=recv_sem, device_id=peer, device_id_type=MESH
        )
        copy.start()
        return copy

    def wait_bytes(ref, sem):
        pltpu.make_async_copy(ref, ref, sem).wait()

    rows_copy = remote(rows_in.at[z_hi], rows_in.at[z_hi], rows_send, rows_sem, z_peer)
    for peer in z_near:
        pl.semaphore_signal(ping_sem, inc=1, device_id=peer, device_id_type=MESH)
    tail_pair = remote(tail.at[0], tail.at[1], tail_send.at[0], tail_sem.at[0], sibling)

    def landing(which, kind, slot):
        tiles_at = pl.ds(0, 256) if which == 0 else pl.ds(256, 128)
        return weights.at[kind, core, tiles_at, pl.ds(slot * 128, 128)]

    def piece(which, kind, holder):
        if which == 0:
            return stage.at[pl.ds(pl.multiple_of(kind * 1024 + holder * 256, 128), 256)]
        return stage.at[pl.ds(pl.multiple_of(2048 + kind * 512 + holder * 128, 128), 128)]

    def send_pieces(which, steps):
        for o in steps:
            for kind, coord, peer in ((0, x, x_peer(o)), (1, y, y_peer(o))):
                src = piece(which, kind, lax.rem(coord + o, 4))
                remote(src, landing(which, kind, 4 - o), w_send, w_sem.at[kind, 4 - o, which], peer)

    send_pieces(0, (2, 1, 3))
    send_pieces(1, (2, 1, 3))
    for o in (2, 1, 3):
        remote(rows_in.at[z_hi], rows.at[4 - o, z_hi], ring_send.at[0], ring_sem.at[0], x_peer(o))
        remote(rows_in.at[z_hi], rows.at[8 - o, z_hi], ring_send.at[0], ring_sem.at[0], y_peer(o))
    for which in range(2):
        for kind, coord in ((0, x), (1, y)):
            src, dst = piece(which, kind, coord), landing(which, kind, 0)
            pltpu.make_async_copy(src, dst, own_sem).start()
            remote(src, dst, pass_send, pass_sem.at[which], sibling)

    tail_pair.wait_recv()
    tail[2] = tail[0] + tail[1]
    tail_all = remote(tail.at[2], tail.at[3], tail_send.at[1], tail_sem.at[1], z_peer)

    rows_copy.wait_recv()
    pl.semaphore_wait(ping_sem, 2)
    for o in (2, 1, 3):
        remote(rows_in.at[1 - z_hi], rows.at[4 - o, 1 - z_hi], ring_send.at[1], ring_sem.at[1], x_peer(o))
        remote(rows_in.at[1 - z_hi], rows.at[8 - o, 1 - z_hi], ring_send.at[1], ring_sem.at[1], y_peer(o))
    rows_own = rows_in[...].reshape(128, 128)

    for which in range(2):
        for slot in (3, 1, 2):
            for kind in range(2):
                block = landing(which, kind, slot)
                wait_bytes(block, w_sem.at[kind, slot, which])
                remote(block, block, pass_send, pass_sem.at[which], sibling)
    tail_all.wait_recv()
    tail_columns = jnp.concatenate([tail[2] + tail[3], jnp.zeros((112, 128), BF16)], axis=0)
    across = (((1,), (1,)), ((), ()))
    tail_part = lax.dot_general(rows_own, tail_columns, across, preferred_element_type=F32)
    wait_bytes(weights.at[0, 0, :, pl.ds(0, 256)], own_sem)
    for half in range(2):
        wait_bytes(rows.at[pl.ds(0, 3)], ring_sem.at[half])

    def put(j, value):
        for draft in range(2):
            for half in range(2):
                first = half * 64 + draft * 32
                send_f32[draft, pl.ds(half * 512 + j, 32, stride=16), :] = value[first : first + 32]

    in_low = z_hi == 0
    wait_bytes(weights.at[0, :, pl.ds(0, 256)], pass_sem.at[0])
    lefts, lows = [], []
    for kind in range(2):
        lhs = jnp.concatenate([rows_own] + [rows[kind * 4 + s].reshape(128, 128) for s in (1, 2, 3)], axis=1)
        lefts.append(lhs)
        part = lax.dot_general(
            lhs, weights[kind, :, 0:256, :].reshape(512, 512), across, preferred_element_type=F32
        )
        for side in range(2):
            for t in range(2):
                column = part[:, side * 256 + t * 128 : side * 256 + (t + 1) * 128]
                put(kind * 6 + side * 3 + t, column)
                if side == 0:
                    lows.append(split_low(column))
    put(13, jnp.where(in_low, lows[1], tail_part))
    put(14, jnp.where(in_low, lows[2], split_low(tail_part)))
    put(15, lows[3])
    wait_bytes(weights.at[0, :, pl.ds(256, 128)], pass_sem.at[1])
    for kind in range(2):
        part = lax.dot_general(
            lefts[kind], weights[kind, :, 256:384, :].reshape(256, 512), across, preferred_element_type=F32
        )
        for side in range(2):
            column = part[:, side * 128 : (side + 1) * 128]
            put(kind * 6 + side * 3 + 2, column)
    put(12, jnp.where(in_low, lows[0], split_low(column)))
    me = z_hi * 32 + loop_id
    for draft in range(2):
        for block in range(4):
            packed = send_f32[draft, pl.ds(block * 256, 256), :].astype(BF16)
            send[draft, pl.ds(block * 16, 16)] = packed.reshape(16, 16, 128)

        def send_sums(to):
            pltpu.make_async_remote_copy(
                src_ref=send.at[draft, to], dst_ref=received.at[draft, me],
                send_sem=sums_send.at[draft], recv_sem=sums_recv.at[draft],
                device_id=(lax.rem(to, 32), lax.div(to, 32) * 2 + core), device_id_type=MESH,
            ).start()

        for half in range(2):
            for o_z, o_y, o_x in offsets(2):
                send_sums(half * 32 + lax.rem(z_lo + o_z, 2) * 16 + lax.rem(y + o_y, 4) * 4 + lax.rem(x + o_x, 4))

            @pl.when(z_hi != half)
            def _():
                send_sums(half * 32 + loop_id)

    keep = pltpu.make_async_copy(send.at[:, me], received.at[:, me], own_sem)
    keep.start()

    for load in loads[2:]:
        load.wait()
    keep.wait()

    n_old = [norm[:, 0:128], norm[:, 128:256]]
    admit_bias = to_column(bias[0:1, :])
    forget_bias = to_column(bias[1:2, :])
    stabilizer = to_column(stab[...])
    q, keys, v, out_gate, forget, admit = [], [], [], [], [], []
    lane = lax.broadcasted_iota(jnp.int32, (24, 128), 1)
    row = lax.broadcasted_iota(jnp.int32, (24, 128), 0)

    def by_head(draft, first, width):
        return [flat[draft, pl.ds(first + i, 8, stride=width), :] for i in range(width)]

    def dot(a, b):
        total = a[0] * b[0]
        for i in range(1, len(a)):
            total = total + a[i] * b[i]
        return jnp.sum(total, axis=1, keepdims=True)

    for draft in range(2):
        wait_bytes(received.at[draft, pl.ds(0, 63)], sums_recv.at[draft])

        tails = None
        for half in range(2):
            for holder in range(4):
                sum_x = sum_y = None
                for lo in range(2):
                    for k in range(4):
                        one_x = received[draft, half * 32 + lo * 16 + k * 4 + holder].astype(F32)
                        one_y = received[draft, half * 32 + lo * 16 + holder * 4 + k].astype(F32)
                        sum_x = one_x if sum_x is None else sum_x + one_x
                        sum_y = one_y if sum_y is None else sum_y + one_y
                if half == 1:
                    tails = sum_x if tails is None else tails + sum_x
                for kind, total in enumerate((sum_x, sum_y)):
                    for side in range(2):
                        j = kind * 6 + side * 3
                        pair, last = total[j : j + 2], total[j + 2 : j + 3]
                        if half == 0 and side == 0:
                            pair = pair + total[12 + kind * 2 : 14 + kind * 2]
                        if half == 1 and side == 1 and kind == 1 and holder == 3:
                            last = last + total[12:13]
                        base = half * 48 + side * 24
                        tiles[pl.ds(base + kind * 8 + 2 * holder, 2), :] = pair
                        tiles[pl.ds(base + 16 + kind * 4 + holder, 1), :] = last

        tail_row = tails[13:14] + tails[14:15]
        for grp in range(4):
            block = tiles[pl.ds(grp * 24, 24), :]
            if grp:
                block = pltpu.roll(block, 4 * grp, 1)
            rolled[pl.ds(grp * 24 + 1, 24), :] = block
            if grp:
                before = rolled[pl.ds(grp * 24, 24), :]
                merged = jnp.where(lane >= 4 * grp, block, before)
                edge = (row == 0) & (lane >= 4 * grp - 4) & (lane < 4 * grp)
                block = jnp.where(edge, jnp.broadcast_to(tail_row, (24, 128)), merged)
            flat[draft, pl.ds(grp * 24, 24), :] = block
        gates = jnp.where(lane[0:1] >= 12, tail_row, rolled[pl.ds(96, 1), :])

        queries_t = flat[draft, 0:16, :].T
        for head in range(8):
            total = jnp.zeros((8, 512), F32)
            for part in range(8):
                block = memory[head, pl.ds(part * 32, 32), :]
                k = (part % 4) * 32
                at = head * 2 + part // 4
                product = queries_t[k : k + 32, at : at + 1] * block
                total = total + jnp.sum(product.reshape(4, 8, 512), axis=0)
            numer[pl.ds(head, 1), :] = jnp.sum(total, axis=0, keepdims=True)

        q.append(by_head(draft, 0, 2))
        keys.append([k * 0.0625 for k in by_head(draft, 16, 2)])
        v.append(by_head(draft, 32, 4))
        out_gate = by_head(draft, 64, 4)
        admit_pre = to_column(gates) + admit_bias
        forget_pre = to_column(gates, 8) + forget_bias
        log_forget = jnp.minimum(forget_pre, 0.0) - jnp.log1p(jnp.exp(-jnp.abs(forget_pre)))
        new_stabilizer = jnp.maximum(log_forget + stabilizer, admit_pre)
        forget.append(jnp.exp(log_forget + stabilizer - new_stabilizer))
        admit.append(jnp.exp(admit_pre - new_stabilizer))
        stabilizer = new_stabilizer

        on_old = forget[0] if draft == 0 else forget[0] * forget[1]
        on_keys = [admit[0]] if draft == 0 else [forget[1] * admit[0], admit[1]]
        on_values = [on_keys[i] * dot(q[draft], keys[i]) for i in range(draft + 1)]
        below = on_old * dot(q[draft], n_old)
        for part in on_values:
            below = below + part
        inverse = 1.0 / jnp.maximum(jnp.abs(below), 1.0)
        hidden = []
        for j in range(4):
            top = on_old * numer[:, pl.ds(j * 128, 128)]
            for i in range(draft + 1):
                top = top + on_values[i] * v[i][j]
            hidden.append(top * inverse)
        square_sum = hidden[0] * hidden[0]
        for j in range(1, 4):
            square_sum = square_sum + hidden[j] * hidden[j]
        mean = jnp.sum(jnp.sum(square_sum, axis=1, keepdims=True), axis=0, keepdims=True) * (1.0 / 4096.0)
        rescale = lax.rsqrt(mean + 1e-06)
        message = [
            hidden[j] * rescale * gain[pl.ds(j, 8, stride=4), :] * jax.nn.sigmoid(out_gate[j]) for j in range(4)
        ]
        readout[draft] = jnp.concatenate(message, axis=0).astype(BF16)

        def send_readout(to):
            pltpu.make_async_remote_copy(
                src_ref=readout.at[draft], dst_ref=gathered.at[draft, loop_id],
                send_sem=gather_send.at[draft], recv_sem=gather_recv.at[draft],
                device_id=(to, grp_id), device_id_type=MESH,
            ).start()

        for to in sorted(range(32), key=lambda d: (min(d % 4, 4 - d % 4) + min(d // 4 % 4, 4 - d // 4 % 4) + d // 16)):
            @pl.when(loop_id != to)
            def _():
                send_readout(to)

    keep = pltpu.make_async_copy(readout, gathered.at[:, loop_id], own_sem)
    keep.start()

    for i in range(2):
        norm_out_ref[0, :, pl.ds(i * 128, 128)] = on_old * n_old[i] + on_keys[0] * keys[0][i] + on_keys[1] * keys[1][i]
    square = (8, 8)
    diagonal = lax.broadcasted_iota(jnp.int32, square, 0) == lax.broadcasted_iota(jnp.int32, square, 1)
    stab_out_ref[...] = jnp.sum(
        jnp.where(diagonal, jnp.broadcast_to(stabilizer, square), 0.0), axis=0, keepdims=True
    )

    for i in range(2):
        for j in range(4):
            scaled[i, :, pl.ds(j * 128, 128)] = on_keys[i] * v[i][j]
    keys_t = (jnp.concatenate([flat[0, 16:32, :], flat[1, 16:32, :]], axis=0) * 0.0625).T
    for head in range(8):
        fade = jnp.broadcast_to(on_old[head : head + 1, :], (32, 512))
        row0, row1 = scaled[0, pl.ds(head, 1), :], scaled[1, pl.ds(head, 1), :]
        for part in range(8):
            k = (part % 4) * 32
            at = head * 2 + part // 4
            k0 = keys_t[k : k + 32, at : at + 1]
            k1 = keys_t[k : k + 32, 16 + at : 17 + at]
            old = memory[head, pl.ds(part * 32, 32), :]
            memory_out_ref[0, head, pl.ds(part * 32, 32), :] = fade * old + k0 * row0 + k1 * row1

    keep.wait()
    for draft in range(2):
        wait_bytes(gathered.at[draft, pl.ds(0, 31)], gather_recv.at[draft])
        for block in range(4):
            piece = gathered[draft, pl.ds(block * 8, 8)].reshape(256, 128)
            gathered_f32[pl.ds(block * 256, 256), :] = piece.astype(F32)
        for j in range(4):
            for head in range(8):
                piece = gathered_f32[pl.ds(j * 8 + head, 32, stride=32), :]
                left[:, pl.ds((head * 4 + j) * 128, 128)] = piece.astype(BF16)
        product = jnp.dot(left[...], out_weight[...], preferred_element_type=F32)
        mixed_ref[draft] = product.astype(BF16)

    rows_copy.wait_send()
    tail_pair.wait_send()
    tail_all.wait_send()
    wait_bytes(weights.at[0, :, :, pl.ds(0, 384)], w_send)
    wait_bytes(weights.at[0], pass_send)
    for half in range(2):
        wait_bytes(rows.at[pl.ds(0, 3)], ring_send.at[half])
    for draft in range(2):
        wait_bytes(send.at[draft, pl.ds(0, 63)], sums_send.at[draft])
        wait_bytes(gathered.at[draft, pl.ds(0, 31)], gather_send.at[draft])


def hand_over_kernel(mixed, memory, norm, stab, mixed_out, memory_out, norm_out, stab_out, sem):
    pairs = [(memory.at[0, head], memory_out.at[0, head]) for head in range(8)]
    pairs += [(mixed, mixed_out), (norm, norm_out), (stab, stab_out)]
    copies = [pltpu.make_async_copy(src, dst, sem.at[i]) for i, (src, dst) in enumerate(pairs)]
    for copy in copies:
        copy.start()
    for copy in copies:
        copy.wait()


def body(inputs, in_weight, gate_bias, memory, normalizer, stabilizer, out_gain, out_weight):
    vmem = pl.BlockSpec(memory_space=pltpu.VMEM)
    hbm = pl.BlockSpec(memory_space=pltpu.HBM)
    dma = pltpu.SemaphoreType.DMA
    out_shape = (
        jax.ShapeDtypeStruct((2, 32, 128), BF16),
        jax.ShapeDtypeStruct(memory.shape, F32),
        jax.ShapeDtypeStruct((1, 8, 256), F32),
        jax.ShapeDtypeStruct((1, 8), F32),
    )
    results = pl.pallas_call(
        exchange_kernel,
        out_shape=out_shape,
        in_specs=[hbm] * 8,
        out_specs=(vmem,) * 4,
        scratch_shapes=[
            pltpu.VMEM((3076, 128), BF16),
            pltpu.VMEM((8, 256, 512), F32),
            pltpu.VMEM((4096, 128), BF16),
            pltpu.VMEM((2, 8), F32),
            pltpu.VMEM((8, 256), F32),
            pltpu.VMEM((1, 8), F32),
            pltpu.VMEM((40, 128), F32),
            pltpu.VMEM((2, 2, 32, 128), BF16),
            pltpu.VMEM((8, 2, 2, 32, 128), BF16),
            pltpu.VMEM((4, 16, 128), BF16),
            pltpu.VMEM((16, 128), F32),
            pltpu.VMEM((2, 2, 384, 512), BF16),
            pltpu.VMEM((2, 1040, 128), F32),
            pltpu.VMEM((2, 64, 16, 128), BF16),
            pltpu.VMEM((2, 64, 16, 128), BF16),
            pltpu.VMEM((96, 128), F32),
            pltpu.VMEM((104, 128), F32),
            pltpu.VMEM((2, 104, 128), F32),
            pltpu.VMEM((8, 512), F32),
            pltpu.VMEM((2, 8, 512), F32),
            pltpu.VMEM((2, 32, 128), BF16),
            pltpu.VMEM((2, 32, 32, 128), BF16),
            pltpu.VMEM((1056, 128), F32),
            pltpu.VMEM((32, 4096), BF16),
            dma((8,)),
            dma,
            dma,
            dma,
            dma((2,)),
            dma((2,)),
            dma((2,)),
            dma((2,)),
            dma,
            dma((2, 4, 2)),
            dma,
            dma((2,)),
            dma((2,)),
            dma((2,)),
            dma((2,)),
            dma((2,)),
            pltpu.SemaphoreType.REGULAR,
        ],
        compiler_params=pltpu.CompilerParams(
            collective_id=0, has_side_effects=True, vmem_limit_bytes=40 * 2**20
        ),
    )(*(
        pltpu.with_memory_space_constraint(operand, pltpu.HBM)
        for operand in (
            inputs, in_weight.T, gate_bias, memory, normalizer, stabilizer, out_gain.reshape(32, 128), out_weight
        )
    ))
    return pl.pallas_call(
        hand_over_kernel,
        out_shape=out_shape,
        in_specs=[vmem] * 4,
        out_specs=(hbm,) * 4,
        scratch_shapes=[dma((11,))],
        compiler_params=pltpu.CompilerParams(vmem_limit_bytes=2 * 2**20),
    )(*results)


def solution(mesh):
    in_specs = (
        P(None, "grp", "loop"),
        P("loop", "grp"),
        P(),
        P(("grp", "loop"), None, None, None),
        P(("grp", "loop"), None, None),
        P(("grp", "loop"), None),
        P(),
        P(None, "loop"),
    )
    out_specs = (
        P(None, "grp", "loop"),
        P(("grp", "loop"), None, None, None),
        P(("grp", "loop"), None, None),
        P(("grp", "loop"), None),
    )
    return jax.shard_map(body, mesh=mesh, in_specs=in_specs, out_specs=out_specs, check_vma=False)
```

```python
import jax
import jax.numpy as jnp
from jax import lax
from jax.experimental import pallas as pl
from jax.experimental.pallas import tpu as pltpu
from jax.sharding import PartitionSpec as P

MESH = pl.DeviceIdType.MESH
F32 = jnp.float32
BF16 = jnp.bfloat16


def split_low(value):
    return value - value.astype(BF16).astype(F32)


def offsets(deep):
    steps = [(o_z, o_y, o_x) for o_z in range(deep) for o_y in range(4) for o_x in range(4)]
    return sorted(steps[1:], key=lambda step: -sum(min(o, 4 - o) for o in step))


def to_column(row, shift=0):
    wide = jnp.broadcast_to(row, (8, row.shape[1]))
    lane = lax.broadcasted_iota(jnp.int32, wide.shape, 1)
    head = lax.broadcasted_iota(jnp.int32, wide.shape, 0)
    return jnp.sum(jnp.where(lane == head + shift, wide, 0.0), axis=1, keepdims=True)


def exchange_kernel(
    inputs_hbm, weight_hbm, bias_hbm, memory_hbm, norm_hbm, stab_hbm, gain_hbm, out_weight_hbm,
    mixed_ref, memory_out_ref, norm_out_ref, stab_out_ref,
    stage, memory, out_weight, bias, norm, stab, gain, rows_in, rows, tail, tail_f32, weights,
    send_f32, send, received, tiles, rolled, flat, numer, scaled, readout, gathered, gathered_f32,
    load_sem, own_sem, rows_send, rows_sem, ring_send, ring_sem, tail_send, tail_sem, w_send, w_sem, pass_send,
    pass_sem, sums_send, sums_recv, gather_send, gather_recv, ping_sem,
):
    loop_id = lax.axis_index("loop")
    grp_id = lax.axis_index("grp")
    x = lax.rem(loop_id, 4)
    y = lax.rem(lax.div(loop_id, 4), 4)
    z_lo = lax.div(loop_id, 16)
    z_hi = lax.div(grp_id, 2)
    core = lax.rem(grp_id, 2)

    def x_peer(o):
        return (z_lo * 16 + y * 4 + lax.rem(x + o, 4), grp_id)

    def y_peer(o):
        return (z_lo * 16 + lax.rem(y + o, 4) * 4 + x, grp_id)

    z_peer = (loop_id, (1 - z_hi) * 2 + core)
    other_lo = (1 - z_lo) * 16 + y * 4 + x
    z_near = [(other_lo, grp_id), (other_lo, (1 - z_hi) * 2 + core)]
    sibling = (loop_id, z_hi * 2 + 1 - core)

    barrier = pltpu.get_barrier_semaphore()
    peers = [x_peer(2), y_peer(2), z_peer] + z_near
    peers += [x_peer(1), x_peer(3), y_peer(1), y_peer(3), sibling]
    for peer in peers:
        pl.semaphore_signal(barrier, inc=1, device_id=peer, device_id_type=MESH)

    loads = [
        pltpu.make_async_copy(src, dst, load_sem.at[i])
        for i, (src, dst) in enumerate((
            (inputs_hbm, rows_in.at[z_hi]),
            (weight_hbm, stage),
            (bias_hbm, bias),
            (stab_hbm, stab),
            (norm_hbm.at[0], norm),
            (gain_hbm, gain.at[pl.ds(0, 32)]),
            (memory_hbm.at[0], memory),
            (out_weight_hbm, out_weight),
        ))
    ]
    for load in loads:
        load.start()

    loads[0].wait()
    loads[1].wait()
    tail_f32[...] = jnp.zeros_like(tail_f32)
    tail_f32[0:4, :] = stage[3072:3076, :].astype(F32)
    tail[0] = pltpu.roll(tail_f32[...], grp_id * 4, 0).astype(BF16)

    pl.semaphore_wait(barrier, len(peers))

    def remote(src, dst, send_sem, recv_sem, peer):
        copy = pltpu.make_async_remote_copy(
            src_ref=src, dst_ref=dst, send_sem=send_sem, recv_sem=recv_sem, device_id=peer, device_id_type=MESH
        )
        copy.start()
        return copy

    def wait_bytes(ref, sem):
        pltpu.make_async_copy(ref, ref, sem).wait()

    rows_copy = remote(rows_in.at[z_hi], rows_in.at[z_hi], rows_send, rows_sem, z_peer)
    for peer in z_near:
        pl.semaphore_signal(ping_sem, inc=1, device_id=peer, device_id_type=MESH)
    tail_pair = remote(tail.at[0], tail.at[1], tail_send.at[0], tail_sem.at[0], sibling)

    def landing(which, kind, slot):
        tiles_at = pl.ds(0, 256) if which == 0 else pl.ds(256, 128)
        return weights.at[kind, core, tiles_at, pl.ds(slot * 128, 128)]

    def piece(which, kind, holder):
        if which == 0:
            return stage.at[pl.ds(pl.multiple_of(kind * 1024 + holder * 256, 128), 256)]
        return stage.at[pl.ds(pl.multiple_of(2048 + kind * 512 + holder * 128, 128), 128)]

    def send_pieces(which, steps):
        for o in steps:
            for kind, coord, peer in ((0, x, x_peer(o)), (1, y, y_peer(o))):
                src = piece(which, kind, lax.rem(coord + o, 4))
                remote(src, landing(which, kind, 4 - o), w_send, w_sem.at[kind, 4 - o, which], peer)

    send_pieces(0, (2, 1, 3))
    send_pieces(1, (2, 1, 3))
    for o in (2, 1, 3):
        remote(rows_in.at[z_hi], rows.at[4 - o, z_hi], ring_send.at[0], ring_sem.at[0], x_peer(o))
        remote(rows_in.at[z_hi], rows.at[8 - o, z_hi], ring_send.at[0], ring_sem.at[0], y_peer(o))
    for which in range(2):
        for kind, coord in ((0, x), (1, y)):
            src, dst = piece(which, kind, coord), landing(which, kind, 0)
            pltpu.make_async_copy(src, dst, own_sem).start()
            remote(src, dst, pass_send, pass_sem.at[which], sibling)

    tail_pair.wait_recv()
    tail[2] = tail[0] + tail[1]
    tail_all = remote(tail.at[2], tail.at[3], tail_send.at[1], tail_sem.at[1], z_peer)

    rows_copy.wait_recv()
    pl.semaphore_wait(ping_sem, 2)
    for o in (2, 1, 3):
        remote(rows_in.at[1 - z_hi], rows.at[4 - o, 1 - z_hi], ring_send.at[1], ring_sem.at[1], x_peer(o))
        remote(rows_in.at[1 - z_hi], rows.at[8 - o, 1 - z_hi], ring_send.at[1], ring_sem.at[1], y_peer(o))
    rows_own = rows_in[...].reshape(128, 128)

    for which in range(2):
        for slot in (3, 1, 2):
            for kind in range(2):
                block = landing(which, kind, slot)
                wait_bytes(block, w_sem.at[kind, slot, which])
                remote(block, block, pass_send, pass_sem.at[which], sibling)
    tail_all.wait_recv()
    tail_columns = jnp.concatenate([tail[2] + tail[3], jnp.zeros((112, 128), BF16)], axis=0)
    across = (((1,), (1,)), ((), ()))
    tail_part = lax.dot_general(rows_own, tail_columns, across, preferred_element_type=F32)
    wait_bytes(weights.at[0, 0, :, pl.ds(0, 256)], own_sem)
    for half in range(2):
        wait_bytes(rows.at[pl.ds(0, 3)], ring_sem.at[half])

    def put(j, value):
        for draft in range(2):
            for half in range(2):
                first = half * 64 + draft * 32
                send_f32[draft, pl.ds(half * 512 + j, 32, stride=16), :] = value[first : first + 32]

    in_low = z_hi == 0
    wait_bytes(weights.at[0, :, pl.ds(0, 256)], pass_sem.at[0])
    lefts, lows = [], []
    for kind in range(2):
        lhs = jnp.concatenate([rows_own] + [rows[kind * 4 + s].reshape(128, 128) for s in (1, 2, 3)], axis=1)
        lefts.append(lhs)
        part = lax.dot_general(
            lhs, weights[kind, :, 0:256, :].reshape(512, 512), across, preferred_element_type=F32
        )
        for side in range(2):
            for t in range(2):
                column = part[:, side * 256 + t * 128 : side * 256 + (t + 1) * 128]
                put(kind * 6 + side * 3 + t, column)
                if side == 0:
                    lows.append(split_low(column))
    put(13, jnp.where(in_low, lows[1], tail_part))
    put(14, jnp.where(in_low, lows[2], split_low(tail_part)))
    put(15, lows[3])
    wait_bytes(weights.at[0, :, pl.ds(256, 128)], pass_sem.at[1])
    for kind in range(2):
        part = lax.dot_general(
            lefts[kind], weights[kind, :, 256:384, :].reshape(256, 512), across, preferred_element_type=F32
        )
        for side in range(2):
            column = part[:, side * 128 : (side + 1) * 128]
            put(kind * 6 + side * 3 + 2, column)
    put(12, jnp.where(in_low, lows[0], split_low(column)))
    me = z_hi * 32 + loop_id
    for draft in range(2):
        for block in range(4):
            packed = send_f32[draft, pl.ds(block * 256, 256), :].astype(BF16)
            send[draft, pl.ds(block * 16, 16)] = packed.reshape(16, 16, 128)

        def send_sums(to):
            pltpu.make_async_remote_copy(
                src_ref=send.at[draft, to], dst_ref=received.at[draft, me],
                send_sem=sums_send.at[draft], recv_sem=sums_recv.at[draft],
                device_id=(lax.rem(to, 32), lax.div(to, 32) * 2 + core), device_id_type=MESH,
            ).start()

        for half in range(2):
            for o_z, o_y, o_x in offsets(2):
                send_sums(half * 32 + lax.rem(z_lo + o_z, 2) * 16 + lax.rem(y + o_y, 4) * 4 + lax.rem(x + o_x, 4))

            @pl.when(z_hi != half)
            def _():
                send_sums(half * 32 + loop_id)

    keep = pltpu.make_async_copy(send.at[:, me], received.at[:, me], own_sem)
    keep.start()

    for load in loads[2:]:
        load.wait()
    keep.wait()

    n_old = [norm[:, 0:128], norm[:, 128:256]]
    admit_bias = to_column(bias[0:1, :])
    forget_bias = to_column(bias[1:2, :])
    stabilizer = to_column(stab[...])
    q, keys, v, out_gate, forget, admit = [], [], [], [], [], []
    lane = lax.broadcasted_iota(jnp.int32, (24, 128), 1)
    row = lax.broadcasted_iota(jnp.int32, (24, 128), 0)

    def by_head(draft, first, width):
        return [flat[draft, pl.ds(first + i, 8, stride=width), :] for i in range(width)]

    def dot(a, b):
        total = a[0] * b[0]
        for i in range(1, len(a)):
            total = total + a[i] * b[i]
        return jnp.sum(total, axis=1, keepdims=True)

    for draft in range(2):
        wait_bytes(received.at[draft, pl.ds(0, 63)], sums_recv.at[draft])

        tails = None
        for half in range(2):
            for holder in range(4):
                sum_x = sum_y = None
                for lo in range(2):
                    for k in range(4):
                        one_x = received[draft, half * 32 + lo * 16 + k * 4 + holder].astype(F32)
                        one_y = received[draft, half * 32 + lo * 16 + holder * 4 + k].astype(F32)
                        sum_x = one_x if sum_x is None else sum_x + one_x
                        sum_y = one_y if sum_y is None else sum_y + one_y
                if half == 1:
                    tails = sum_x if tails is None else tails + sum_x
                for kind, total in enumerate((sum_x, sum_y)):
                    for side in range(2):
                        j = kind * 6 + side * 3
                        pair, last = total[j : j + 2], total[j + 2 : j + 3]
                        if half == 0 and side == 0:
                            pair = pair + total[12 + kind * 2 : 14 + kind * 2]
                        if half == 1 and side == 1 and kind == 1 and holder == 3:
                            last = last + total[12:13]
                        base = half * 48 + side * 24
                        tiles[pl.ds(base + kind * 8 + 2 * holder, 2), :] = pair
                        tiles[pl.ds(base + 16 + kind * 4 + holder, 1), :] = last

        tail_row = tails[13:14] + tails[14:15]
        for grp in range(4):
            block = tiles[pl.ds(grp * 24, 24), :]
            if grp:
                block = pltpu.roll(block, 4 * grp, 1)
            rolled[pl.ds(grp * 24 + 1, 24), :] = block
            if grp:
                before = rolled[pl.ds(grp * 24, 24), :]
                merged = jnp.where(lane >= 4 * grp, block, before)
                edge = (row == 0) & (lane >= 4 * grp - 4) & (lane < 4 * grp)
                block = jnp.where(edge, jnp.broadcast_to(tail_row, (24, 128)), merged)
            flat[draft, pl.ds(grp * 24, 24), :] = block
        gates = jnp.where(lane[0:1] >= 12, tail_row, rolled[pl.ds(96, 1), :])

        queries_t = flat[draft, 0:16, :].T
        for head in range(8):
            total = jnp.zeros((8, 512), F32)
            for part in range(8):
                block = memory[head, pl.ds(part * 32, 32), :]
                k = (part % 4) * 32
                at = head * 2 + part // 4
                product = queries_t[k : k + 32, at : at + 1] * block
                total = total + jnp.sum(product.reshape(4, 8, 512), axis=0)
            numer[pl.ds(head, 1), :] = jnp.sum(total, axis=0, keepdims=True)

        q.append(by_head(draft, 0, 2))
        keys.append([k * 0.0625 for k in by_head(draft, 16, 2)])
        v.append(by_head(draft, 32, 4))
        out_gate = by_head(draft, 64, 4)
        admit_pre = to_column(gates) + admit_bias
        forget_pre = to_column(gates, 8) + forget_bias
        log_forget = jnp.minimum(forget_pre, 0.0) - jnp.log1p(jnp.exp(-jnp.abs(forget_pre)))
        new_stabilizer = jnp.maximum(log_forget + stabilizer, admit_pre)
        forget.append(jnp.exp(log_forget + stabilizer - new_stabilizer))
        admit.append(jnp.exp(admit_pre - new_stabilizer))
        stabilizer = new_stabilizer

        on_old = forget[0] if draft == 0 else forget[0] * forget[1]
        on_keys = [admit[0]] if draft == 0 else [forget[1] * admit[0], admit[1]]
        on_values = [on_keys[i] * dot(q[draft], keys[i]) for i in range(draft + 1)]
        below = on_old * dot(q[draft], n_old)
        for part in on_values:
            below = below + part
        inverse = 1.0 / jnp.maximum(jnp.abs(below), 1.0)
        hidden = []
        for j in range(4):
            top = on_old * numer[:, pl.ds(j * 128, 128)]
            for i in range(draft + 1):
                top = top + on_values[i] * v[i][j]
            hidden.append(top * inverse)
        square_sum = hidden[0] * hidden[0]
        for j in range(1, 4):
            square_sum = square_sum + hidden[j] * hidden[j]
        mean = jnp.sum(jnp.sum(square_sum, axis=1, keepdims=True), axis=0, keepdims=True) * (1.0 / 4096.0)
        rescale = lax.rsqrt(mean + 1e-06)
        message = [
            hidden[j] * rescale * gain[pl.ds(j, 8, stride=4), :] * jax.nn.sigmoid(out_gate[j]) for j in range(4)
        ]
        readout[draft] = jnp.concatenate(message, axis=0).astype(BF16)

        def send_readout(to):
            pltpu.make_async_remote_copy(
                src_ref=readout.at[draft], dst_ref=gathered.at[draft, loop_id],
                send_sem=gather_send.at[draft], recv_sem=gather_recv.at[draft],
                device_id=(to, grp_id), device_id_type=MESH,
            ).start()

        for to in sorted(range(32), key=lambda d: (min(d % 4, 4 - d % 4) + min(d // 4 % 4, 4 - d // 4 % 4) + d // 16)):
            @pl.when(loop_id != to)
            def _():
                send_readout(to)

    keep = pltpu.make_async_copy(readout, gathered.at[:, loop_id], own_sem)
    keep.start()

    for i in range(2):
        norm_out_ref[0, :, pl.ds(i * 128, 128)] = on_old * n_old[i] + on_keys[0] * keys[0][i] + on_keys[1] * keys[1][i]
    square = (8, 8)
    diagonal = lax.broadcasted_iota(jnp.int32, square, 0) == lax.broadcasted_iota(jnp.int32, square, 1)
    stab_out_ref[...] = jnp.sum(
        jnp.where(diagonal, jnp.broadcast_to(stabilizer, square), 0.0), axis=0, keepdims=True
    )

    for i in range(2):
        for j in range(4):
            scaled[i, :, pl.ds(j * 128, 128)] = on_keys[i] * v[i][j]
    keys_t = (jnp.concatenate([flat[0, 16:32, :], flat[1, 16:32, :]], axis=0) * 0.0625).T
    for head in range(8):
        fade = jnp.broadcast_to(on_old[head : head + 1, :], (32, 512))
        row0, row1 = scaled[0, pl.ds(head, 1), :], scaled[1, pl.ds(head, 1), :]
        for part in range(8):
            k = (part % 4) * 32
            at = head * 2 + part // 4
            k0 = keys_t[k : k + 32, at : at + 1]
            k1 = keys_t[k : k + 32, 16 + at : 17 + at]
            old = memory[head, pl.ds(part * 32, 32), :]
            memory_out_ref[0, head, pl.ds(part * 32, 32), :] = fade * old + k0 * row0 + k1 * row1

    keep.wait()
    for draft in range(2):
        wait_bytes(gathered.at[draft, pl.ds(0, 31)], gather_recv.at[draft])
        for block in range(4):
            piece = gathered[draft, pl.ds(block * 8, 8)].reshape(256, 128)
            gathered_f32[pl.ds(block * 256, 256), :] = piece.astype(F32)
        product = None
        for half in range(2):
            pieces_of_half = [
                gathered_f32[pl.ds(j * 8 + head, 32, stride=32), :].astype(BF16)
                for head in range(half * 4, half * 4 + 4)
                for j in range(4)
            ]
            term = jnp.dot(
                jnp.concatenate(pieces_of_half, axis=1), out_weight[pl.ds(half * 2048, 2048), :],
                preferred_element_type=F32,
            )
            product = term if product is None else product + term
        mixed_ref[draft] = product.astype(BF16)

    rows_copy.wait_send()
    tail_pair.wait_send()
    tail_all.wait_send()
    wait_bytes(weights.at[0, :, :, pl.ds(0, 384)], w_send)
    wait_bytes(weights.at[0], pass_send)
    for half in range(2):
        wait_bytes(rows.at[pl.ds(0, 3)], ring_send.at[half])
    for draft in range(2):
        wait_bytes(send.at[draft, pl.ds(0, 63)], sums_send.at[draft])
        wait_bytes(gathered.at[draft, pl.ds(0, 31)], gather_send.at[draft])


def hand_over_kernel(mixed, memory, norm, stab, mixed_out, memory_out, norm_out, stab_out, sem):
    pairs = [(memory.at[0, head], memory_out.at[0, head]) for head in range(8)]
    pairs += [(mixed, mixed_out), (norm, norm_out), (stab, stab_out)]
    copies = [pltpu.make_async_copy(src, dst, sem.at[i]) for i, (src, dst) in enumerate(pairs)]
    for copy in copies:
        copy.start()
    for copy in copies:
        copy.wait()


def body(inputs, in_weight, gate_bias, memory, normalizer, stabilizer, out_gain, out_weight):
    vmem = pl.BlockSpec(memory_space=pltpu.VMEM)
    hbm = pl.BlockSpec(memory_space=pltpu.HBM)
    dma = pltpu.SemaphoreType.DMA
    out_shape = (
        jax.ShapeDtypeStruct((2, 32, 128), BF16),
        jax.ShapeDtypeStruct(memory.shape, F32),
        jax.ShapeDtypeStruct((1, 8, 256), F32),
        jax.ShapeDtypeStruct((1, 8), F32),
    )
    results = pl.pallas_call(
        exchange_kernel,
        out_shape=out_shape,
        in_specs=[hbm] * 8,
        out_specs=(vmem,) * 4,
        scratch_shapes=[
            pltpu.VMEM((3076, 128), BF16),
            pltpu.VMEM((8, 256, 512), F32),
            pltpu.VMEM((4096, 128), BF16),
            pltpu.VMEM((2, 8), F32),
            pltpu.VMEM((8, 256), F32),
            pltpu.VMEM((1, 8), F32),
            pltpu.VMEM((40, 128), F32),
            pltpu.VMEM((2, 2, 32, 128), BF16),
            pltpu.VMEM((8, 2, 2, 32, 128), BF16),
            pltpu.VMEM((4, 16, 128), BF16),
            pltpu.VMEM((16, 128), F32),
            pltpu.VMEM((2, 2, 384, 512), BF16),
            pltpu.VMEM((2, 1040, 128), F32),
            pltpu.VMEM((2, 64, 16, 128), BF16),
            pltpu.VMEM((2, 64, 16, 128), BF16),
            pltpu.VMEM((96, 128), F32),
            pltpu.VMEM((104, 128), F32),
            pltpu.VMEM((2, 104, 128), F32),
            pltpu.VMEM((8, 512), F32),
            pltpu.VMEM((2, 8, 512), F32),
            pltpu.VMEM((2, 32, 128), BF16),
            pltpu.VMEM((2, 32, 32, 128), BF16),
            pltpu.VMEM((1056, 128), F32),
            dma((8,)),
            dma,
            dma,
            dma,
            dma((2,)),
            dma((2,)),
            dma((2,)),
            dma((2,)),
            dma,
            dma((2, 4, 2)),
            dma,
            dma((2,)),
            dma((2,)),
            dma((2,)),
            dma((2,)),
            dma((2,)),
            pltpu.SemaphoreType.REGULAR,
        ],
        compiler_params=pltpu.CompilerParams(
            collective_id=0, has_side_effects=True, vmem_limit_bytes=40 * 2**20
        ),
    )(*(
        pltpu.with_memory_space_constraint(operand, pltpu.HBM)
        for operand in (
            inputs, in_weight.T, gate_bias, memory, normalizer, stabilizer, out_gain.reshape(32, 128), out_weight
        )
    ))
    return pl.pallas_call(
        hand_over_kernel,
        out_shape=out_shape,
        in_specs=[vmem] * 4,
        out_specs=(hbm,) * 4,
        scratch_shapes=[dma((11,))],
        compiler_params=pltpu.CompilerParams(vmem_limit_bytes=2 * 2**20),
    )(*results)


def solution(mesh):
    in_specs = (
        P(None, "grp", "loop"),
        P("loop", "grp"),
        P(),
        P(("grp", "loop"), None, None, None),
        P(("grp", "loop"), None, None),
        P(("grp", "loop"), None),
        P(),
        P(None, "loop"),
    )
    out_specs = (
        P(None, "grp", "loop"),
        P(("grp", "loop"), None, None, None),
        P(("grp", "loop"), None, None),
        P(("grp", "loop"), None),
    )
    return jax.shard_map(body, mesh=mesh, in_specs=in_specs, out_specs=out_specs, check_vma=False)
```
